128 devices in a mesh: img: 64 (over z, y, x), mdl: 2 (over core).
Axes of the slice: x: 4, y: 4, z: 4, core: 2. Of those that a mesh axis runs over, the one named last changes fastest.
Arguments:
- tokens: bfloat16 [512, 196, 1024], P('img', None, 'mdl'), may hold values from -16 to 16
- image_row: int32 [512], replicated, may hold values from 0 to 511, as said below
- views: int32 [64, 16], replicated, may hold values from 0 to 511, as said below
- pairs: int32 [64, 8, 2], P('img'), may hold values from 0 to 15, as said below
- pair_count: int32 [64], P('img'), may hold values from 4 to 8, as said below
- w_query: bfloat16 [1024, 1024], P(None, 'mdl'), may hold values from -0.1875 to 0.1875
- w_key: bfloat16 [1024, 1024], P(None, 'mdl'), may hold values from -0.1875 to 0.1875
- w_value: bfloat16 [1024, 1024], P(None, 'mdl'), may hold values from -0.1875 to 0.1875
- w_out: bfloat16 [1024, 1024], P('mdl'), may hold values from -0.1875 to 0.1875
- head_in: bfloat16 [1024, 256], P('mdl'), may hold values from -0.1875 to 0.1875
- head_mid: bfloat16 [256, 256], replicated, may hold values from -0.375 to 0.375
- head_last: bfloat16 [4, 256], replicated, may hold values from -0.375 to 0.375
Outputs:
- joined: float32 [512, 3, 196], P('img')
- weight_total: float32 [512, 196], P('img')
The draws below stay inside these ranges and needn't reach their ends.
Inputs may be any that keep to these rules, and one draw needn't show every extreme that they name: `image_row`: a permutation of the 512 storage rows. `views`: each row holds 16 distinct image ids; at most 1 of one row's images are stored on one index of img, and some index of img stores exactly 1 of them. `pairs`: the two entries of a pair differ. `pair_count`: the live pairs are the leading ones; some pair device has 8.
All inputs are finite; a program needn't handle non-finite values.
Results may differ from the reference program's by a relative error of at most 0.025.
Values may be sent and summed in bfloat16 or wider, within the bound.
No kernel may reach another device: no remote copies, remote signals or barrier semaphores. Data moves between devices by JAX's collectives and lax.ppermute only.
A program may use at most 128 MiB of HBM per device.

```python
import jax
import jax.numpy as jnp
from jax import lax

D = 1024
HEADS = 16
HEAD_DIM = 64
TOK = 196
HID = 256
IMG_DEV = 8
PAIR_CAP = 8
VIEW_CAP = 16
IMAGES = 512
N_IMG = 64


def storage_order(key):
    return jax.random.permutation(jax.random.fold_in(key, 101), IMAGES).astype(jnp.int32)


def draw_image_row(key, part):
    return storage_order(key)


def draw_views(key, part):
    order_rows = storage_order(key)
    inverse = jnp.argsort(order_rows).astype(jnp.int32)
    key = jax.random.fold_in(key, 3)
    key_owner, key_device, key_base = jax.random.split(key, 3)
    owner_perm = jax.random.permutation(key_owner, N_IMG).astype(jnp.int32)
    device_perm = jax.random.permutation(key_device, N_IMG).astype(jnp.int32)
    base_rows = jax.random.randint(key_base, (N_IMG, N_IMG), 0, IMG_DEV).astype(jnp.int32)
    slot_index = jnp.arange(VIEW_CAP, dtype=jnp.int32)
    owners = owner_perm[(device_perm[:, None] + slot_index[None, :]) % N_IMG]
    local_slot = (base_rows[:, slot_index % N_IMG] + slot_index[None, :] // N_IMG) % IMG_DEV
    return inverse[owners * IMG_DEV + local_slot].astype(jnp.int32)


def draw_pairs(key, part):
    key = jax.random.fold_in(key, 7)
    key_first, key_step = jax.random.split(key)
    shift_bit = jax.random.randint(key_first, (N_IMG, PAIR_CAP), 0, 2)
    first_view = (2 * jnp.arange(PAIR_CAP, dtype=jnp.int32)[None, :] + shift_bit) % VIEW_CAP
    second_view = (first_view + jax.random.randint(key_step, (N_IMG, PAIR_CAP), 1, VIEW_CAP)) % VIEW_CAP
    return jnp.stack([first_view, second_view], axis=-1).astype(jnp.int32)


def draw_pair_count(key, part):
    key = jax.random.fold_in(key, 9)
    key_one, key_full = jax.random.split(key)
    lowest = PAIR_CAP // 2
    counts = jax.random.randint(key_one, (N_IMG,), lowest, PAIR_CAP + 1)
    full_device = jax.random.randint(key_full, (), 0, N_IMG)
    counts = jnp.where(jnp.arange(N_IMG) == full_device, PAIR_CAP, counts)
    return counts.astype(jnp.int32)


def draw_tokens(key, part):
    key = jax.random.fold_in(key, 5)
    key_value, key_column, key_row = jax.random.split(key, 3)
    rising = 0.2 * 10.0 ** (jnp.arange(D, dtype=jnp.float32) / D)
    columns = rising * jax.random.uniform(key_column, (D,), minval=0.7, maxval=1.4)
    row_scale = jax.random.uniform(key_row, (IMAGES, TOK, 1), minval=0.7, maxval=1.4)
    entries = jnp.clip(jax.random.normal(key_value, (IMAGES, TOK, D)), -4.0, 4.0)
    return (entries * row_scale * columns).astype(jnp.bfloat16)


def shard_levels(own_key, shape, pieces, least, largest):
    level, own = 1.0, jax.random.fold_in(own_key, 6)
    for position, shards_of in pieces:
        heights = jnp.exp(jax.random.uniform(jax.random.fold_in(own, position), (shards_of,), jnp.float32, least / len(pieces), largest / len(pieces)))
        level = level * jnp.repeat(heights, shape[position] // shards_of).reshape([-1 if axis == position else 1 for axis in range(len(shape))])
    return level


def bell_draw(rng, extent, spread, limit, cuts=(), kind=jnp.bfloat16):
    level = shard_levels(rng, extent, cuts, -0.22, 0.18) if cuts else 1.0
    values = jax.random.normal(rng, extent, jnp.float32) * spread * level
    return jnp.minimum(jnp.maximum(values, -limit), limit).astype(kind)


def setup_inputs(seed: int = 0) -> dict:
    key_of = jax.random.split(jax.random.key(seed), 13)
    return {
        "tokens": draw_tokens(jax.random.fold_in(key_of[12], 71), 0),
        "image_row": draw_image_row(jax.random.fold_in(key_of[12], 71), 0),
        "views": draw_views(jax.random.fold_in(key_of[12], 71), 0),
        "pairs": draw_pairs(jax.random.fold_in(key_of[12], 71), 0),
        "pair_count": draw_pair_count(jax.random.fold_in(key_of[12], 71), 0),
        "w_query": bell_draw(key_of[5], (D, D), D ** -0.5, 0.1875, ((1, 2),)),
        "w_key": bell_draw(key_of[6], (D, D), D ** -0.5, 0.1875, ((1, 2),)),
        "w_value": bell_draw(key_of[7], (D, D), D ** -0.5, 0.1875, ((1, 2),)),
        "w_out": bell_draw(key_of[8], (D, D), D ** -0.5, 0.1875, ((0, 2),)),
        "head_in": bell_draw(key_of[9], (D, HID), D ** -0.5, 0.1875, ((0, 2),)),
        "head_mid": bell_draw(key_of[10], (HID, HID), HID ** -0.5, 0.375),
        "head_last": bell_draw(key_of[11], (4, HID), HID ** -0.5, 0.375),
    }


def reference(tokens, image_row, views, pairs, pair_count, w_query, w_key, w_value, w_out, head_in, head_mid, head_last):
    flat_rows = tokens.reshape(IMAGES * TOK, D)

    def project(weight):
        return jnp.dot(flat_rows, weight, preferred_element_type=jnp.float32).astype(jnp.bfloat16).reshape(IMAGES, TOK, D)
    queries = project(w_query)
    keys_all = project(w_key)
    values_all = project(w_value)
    slot_pair = jnp.repeat(jnp.arange(PAIR_CAP, dtype=jnp.int32), 2)
    slot_total = 2 * PAIR_CAP

    def one_device(inputs):
        device_views, device_pairs, device_count = inputs
        stored = image_row[device_views]
        query_rows = stored[device_pairs.reshape(slot_total)]
        key_rows = stored[device_pairs[:, ::-1].reshape(slot_total)]
        live = (slot_pair < device_count).astype(jnp.float32)
        query_heads = queries[query_rows].astype(jnp.float32).reshape(slot_total, TOK, HEADS, HEAD_DIM)
        key_heads = keys_all[key_rows].astype(jnp.float32).reshape(slot_total, TOK, HEADS, HEAD_DIM)
        value_heads = values_all[key_rows].astype(jnp.float32).reshape(slot_total, TOK, HEADS, HEAD_DIM)
        scores = jnp.einsum('sqhd,skhd->shqk', query_heads, key_heads) * HEAD_DIM ** (-0.5)
        weights = jnp.exp(scores)
        probs = (weights / lax.optimization_barrier(jnp.sum(weights, axis=-1, keepdims=True))).astype(jnp.bfloat16)
        attended = jnp.einsum('shqk,skhd->sqhd', probs.astype(jnp.float32), value_heads)
        attended = attended.astype(jnp.bfloat16).reshape(slot_total * TOK, D)
        residual = tokens[query_rows].reshape(slot_total * TOK, D).astype(jnp.float32)
        mixed = residual + jnp.dot(attended, w_out, preferred_element_type=jnp.float32)
        mean_row = lax.optimization_barrier(jnp.mean(mixed, axis=-1, keepdims=True))
        square_row = lax.optimization_barrier(jnp.mean(mixed * mixed, axis=-1, keepdims=True))
        normed = ((mixed - mean_row) * lax.rsqrt(square_row - mean_row * mean_row + 1e-05)).astype(jnp.bfloat16)
        hidden = jax.nn.gelu(jnp.dot(normed, head_in, preferred_element_type=jnp.float32)).astype(jnp.bfloat16)
        inner = jax.nn.gelu(jnp.dot(hidden, head_mid, preferred_element_type=jnp.float32)).astype(jnp.bfloat16)
        head_out = jnp.einsum('sth,ch->sct', inner.reshape(slot_total, TOK, HID).astype(jnp.float32), head_last.astype(jnp.float32))
        points = head_out[:, :3, :]
        confidence = (1.0 + jax.nn.softplus(head_out[:, 3, :])) * live[:, None]
        weighted = points * confidence[:, None, :]
        return (weighted, confidence, query_rows)
    weighted, confidence, targets = lax.map(one_device, (views, pairs, pair_count))
    weighted = weighted.reshape(N_IMG * slot_total, 3, TOK)
    confidence = confidence.reshape(N_IMG * slot_total, TOK)
    targets = targets.reshape(N_IMG * slot_total)
    numerator = jax.ops.segment_sum(weighted, targets, num_segments=IMAGES)
    weight_total = jax.ops.segment_sum(confidence, targets, num_segments=IMAGES)
    joined = numerator / jnp.maximum(weight_total, 1.0)[:, None, :]
    return (joined, weight_total)
```

```python
import functools

import jax
import jax.numpy as jnp
import numpy as np
from jax import lax
from jax.experimental import pallas as pl
from jax.experimental.pallas import tpu as pltpu
from jax.sharding import PartitionSpec as P

D = 1024
HALF = 512
HEAD_DIM = 64
TOK = 196
STEPS = 13
GROUPS = 16
PAD_TOK = STEPS * GROUPS
LANES = 128
BF = jnp.bfloat16
F32 = jnp.float32
MIB = 1 << 20


def spread_kernel(tokens_ref, pairs_ref, perm_ref, out_ref, block):
    for pair_step in range(7):
        if pair_step < 6:
            rows = tokens_ref[:, pair_step * 32 : pair_step * 32 + 32, :]
        else:
            block[...] = jnp.zeros_like(block)
            block[:, 0 : TOK - 192, :] = tokens_ref[:, 192:TOK, :]
            block[:, 16:32, :] = jnp.broadcast_to(pairs_ref[...].reshape(1, 1, HALF), (8, 16, HALF))
            rows = block[...]
        moved = jnp.dot(perm_ref[...], rows.reshape(256, HALF), preferred_element_type=F32)
        moved = moved.astype(BF).reshape(16, 16, HALF)
        for group in range(4):
            out_ref[:, group, pair_step * 16 : pair_step * 16 + 16, :] = moved[
                :, :, group * LANES : (group + 1) * LANES
            ]


def spread(tokens, pair_lanes, perm):
    return pl.pallas_call(
        spread_kernel,
        out_shape=jax.ShapeDtypeStruct((16, 4, 112, LANES), BF),
        scratch_shapes=[pltpu.VMEM((8, 32, HALF), BF)],
        compiler_params=pltpu.CompilerParams(vmem_limit_bytes=32 * MIB),
    )(tokens, pair_lanes, perm)


def select_kernel(pieces_ref, rows_ref, out_ref, images):
    for pair_step in range(7):
        tile = pieces_ref[:, pair_step * 16 : pair_step * 16 + 16, :].astype(F32)
        tile = tile.reshape(64, 2, 8, LANES)
        for half in range(2):
            step = 2 * pair_step + half
            if step < STEPS:
                images[:, step * LANES : (step + 1) * LANES] = (
                    tile[:, half].reshape(512, LANES).astype(BF)
                )
    for part in range(4):
        rows = slice(part * 256, part * 256 + 256)
        hit = rows_ref[rows, :] == lax.broadcasted_iota(jnp.int32, (256, 512), 1)
        chosen = jnp.where(hit, 1.0, 0.0).astype(BF)
        out_ref[rows, :] = jnp.dot(chosen, images[...], preferred_element_type=F32).astype(BF)


def select(pieces, rows):
    return pl.pallas_call(
        select_kernel,
        out_shape=jax.ShapeDtypeStruct((1024, STEPS * LANES), BF),
        scratch_shapes=[pltpu.VMEM((512, STEPS * LANES), BF)],
        compiler_params=pltpu.CompilerParams(vmem_limit_bytes=40 * MIB),
    )(pieces, rows)


def pair_kernel(
    live_ref,
    pieces_ref,
    perm_ref,
    wq0,
    wq1,
    wk0,
    wk1,
    wv0,
    wv1,
    wo0,
    wo1,
    hin0,
    hin1,
    hmid,
    hlast,
    out_ref,
    x_ref,
    q_ref,
    k_ref,
    v_ref,
    att_ref,
):
    pair = pl.program_id(0)

    @pl.when(pair == 0)
    def _():
        for step in range(STEPS):
            lanes = slice(step * LANES, (step + 1) * LANES)
            columns = []
            for core in range(2):
                for group in range(4):
                    tile = pieces_ref[:, group, core, :, lanes].astype(F32)
                    columns.append(tile.reshape(128, LANES).astype(BF))
            rows = jnp.concatenate(columns, axis=1)
            moved = jnp.dot(perm_ref[...], rows, preferred_element_type=F32).astype(BF)
            x_ref[:, step * 16 : step * 16 + 16, :] = moved.reshape(8, 16, D)

    out_ref[...] = jnp.zeros_like(out_ref)

    @pl.when(pair < live_ref[0])
    def _():
        rows = 2 * PAD_TOK
        x = x_ref[pl.ds(2 * pair, 2)].reshape(rows, D)
        for half, (wq, wk, wv) in enumerate(((wq0, wk0, wv0), (wq1, wk1, wv1))):
            cols = slice(half * HALF, (half + 1) * HALF)
            q = jnp.dot(x, wq[...], preferred_element_type=F32).astype(BF)
            q_ref[:, cols] = q * jnp.asarray(HEAD_DIM**-0.5, BF)
            k_ref[:, cols] = jnp.dot(x, wk[...], preferred_element_type=F32).astype(BF)
            v_ref[:, cols] = jnp.dot(x, wv[...], preferred_element_type=F32).astype(BF)

        first = lax.broadcasted_iota(jnp.int32, (PAD_TOK, LANES), 1) < HEAD_DIM
        key_ok = lax.broadcasted_iota(jnp.int32, (rows, PAD_TOK), 1) < TOK

        def heads(index, carry):
            cols = pl.ds(pl.multiple_of(index * LANES, LANES), LANES)
            for slot in range(2):
                mine = slice(slot * PAD_TOK, (slot + 1) * PAD_TOK)
                other = slice((1 - slot) * PAD_TOK, (2 - slot) * PAD_TOK)
                q = q_ref[mine, cols]
                none = jnp.zeros_like(q)
                both = jnp.concatenate([jnp.where(first, q, none), jnp.where(first, none, q)], axis=0)
                scores = lax.dot_general(
                    both, k_ref[other, cols], (((1,), (1,)), ((), ())), preferred_element_type=F32
                )
                scores = jnp.where(key_ok, scores, -jnp.inf)
                weights = jnp.exp(scores - jnp.max(scores, axis=1, keepdims=True))
                probs = weights * (1.0 / jnp.sum(weights, axis=1, keepdims=True))
                got = jnp.dot(probs.astype(BF), v_ref[other, cols], preferred_element_type=F32)
                att_ref[mine, cols] = jnp.where(first, got[:PAD_TOK], got[PAD_TOK:]).astype(BF)
            return carry

        lax.fori_loop(0, D // LANES, heads, 0)

        mixed = x.astype(F32) + jnp.dot(att_ref[:, :HALF], wo0[...], preferred_element_type=F32)
        mixed = mixed + jnp.dot(att_ref[:, HALF:], wo1[...], preferred_element_type=F32)
        mean = jnp.sum(mixed, axis=1, keepdims=True) * (1.0 / D)
        square = jnp.sum(mixed * mixed, axis=1, keepdims=True) * (1.0 / D)
        normed = ((mixed - mean) * lax.rsqrt(square - mean * mean + 1e-05)).astype(BF)
        hidden = jnp.dot(normed[:, :HALF], hin0[...], preferred_element_type=F32)
        hidden = hidden + jnp.dot(normed[:, HALF:], hin1[...], preferred_element_type=F32)
        hidden = jax.nn.gelu(hidden).astype(BF)
        inner = jnp.dot(hidden, hmid[...], preferred_element_type=F32)
        inner = jax.nn.gelu(inner).astype(BF)
        for slot in range(2):
            last = lax.dot_general(
                hlast[...],
                inner[slot * PAD_TOK : (slot + 1) * PAD_TOK],
                (((1,), (1,)), ((), ())),
                preferred_element_type=F32,
            )
            logit = last[3:4, :]
            confidence = 1.0 + jnp.maximum(logit, 0.0) + jnp.log1p(jnp.exp(-jnp.abs(logit)))
            is_conf = lax.broadcasted_iota(jnp.int32, last.shape, 0) == 3
            result = jnp.where(is_conf, 1.0, last) * confidence
            out_ref[slot, :, 0:TOK] = result[:, 0:TOK]


def pair_heads(live, pieces, perm, weights):
    whole = lambda a: pl.BlockSpec(a.shape, lambda i, n=a.ndim: (0,) * n)
    rows = 2 * PAD_TOK
    return pl.pallas_call(
        pair_kernel,
        grid=(4,),
        in_specs=[pl.BlockSpec(memory_space=pltpu.SMEM)] + [whole(a) for a in (pieces, perm, *weights)],
        out_specs=pl.BlockSpec((2, 4, 256), lambda i: (i, 0, 0)),
        out_shape=jax.ShapeDtypeStruct((8, 4, 256), F32),
        scratch_shapes=[
            pltpu.VMEM((8, PAD_TOK, D), BF),
            pltpu.VMEM((rows, D), BF),
            pltpu.VMEM((rows, D), BF),
            pltpu.VMEM((rows, D), BF),
            pltpu.VMEM((rows, D), BF),
        ],
        compiler_params=pltpu.CompilerParams(
            vmem_limit_bytes=56 * MIB, dimension_semantics=("arbitrary",)
        ),
    )(live, pieces, perm, *weights)


def local(
    tokens,
    image_row,
    views,
    pairs,
    pair_count,
    w_query,
    w_key,
    w_value,
    w_out,
    head_in,
    head_mid,
    head_last,
):
    own = lax.axis_index("img")
    core = lax.axis_index("mdl")
    groups = lax.axis_size("img")

    out_row = np.arange(256)
    source = (out_row % 8) * 32 + (out_row // 8 % 2) * 16 + out_row // 16
    spread_perm = jnp.asarray(np.arange(256)[None, :] == source[:, None], BF)
    pair_lanes = jnp.tile(jnp.pad(pairs.reshape(1, 16).astype(BF), ((0, 0), (0, 112))), (1, 4))
    outgoing = spread(tokens, pair_lanes, spread_perm).reshape(64, 112, LANES)
    pieces = lax.all_to_all(outgoing, "img", split_axis=0, concat_axis=0, tiled=True)

    swap = lambda a: lax.ppermute(a, "mdl", [(0, 1), (1, 0)])
    q_other, k_other, v_other, o_other, h_other = (
        swap(a) for a in (w_query, w_key, w_value, w_out, head_in)
    )
    low = core == 0
    hin0 = jnp.where(low, head_in, h_other)
    hin1 = jnp.where(low, h_other, head_in)

    is_image = views[:, :, None] == jnp.arange(image_row.shape[0])
    stored = jnp.sum(jnp.where(is_image, image_row, 0), axis=2)

    all_pairs = pieces[:, 104, :16].astype(jnp.int32)
    is_view = all_pairs[:, :, None] == jnp.arange(16)
    rows = jnp.sum(jnp.where(is_view, stored[:, None, :], 0), axis=2)
    chosen = select(pieces, rows.reshape(1024, 1)).reshape(128, 8, STEPS * LANES)
    arrived = lax.all_to_all(chosen, ("img", "mdl"), split_axis=0, concat_axis=0, tiled=True)

    out_row = np.arange(128)
    source = (out_row % 16) * 8 + out_row // 16
    pair_perm = jnp.asarray(np.arange(128)[None, :] == source[:, None], BF)
    live = jnp.clip(pair_count - 4 * core, 0, 4)
    results = pair_heads(
        live,
        arrived.reshape(GROUPS, 4, 2, 8, STEPS * LANES),
        pair_perm,
        (w_query, q_other, w_key, k_other, w_value, v_other, w_out, o_other, hin0, hin1, head_mid, head_last),
    )

    my_rows = lax.dynamic_index_in_dim(rows, own, 0, keepdims=False)
    my_rows = lax.dynamic_slice_in_dim(my_rows, 8 * core, 8, 0)
    to_owner = (my_rows[None, :] // 8 == jnp.arange(groups)[:, None]).astype(F32)
    sums = jnp.dot(to_owner, results.reshape(8, 1024), precision=lax.Precision.HIGHEST)
    sums = jnp.broadcast_to(sums.astype(BF).reshape(64, 1, 8, LANES), (64, 2, 8, LANES))
    back = lax.all_to_all(
        sums.reshape(128, 8, LANES), ("img", "mdl"), split_axis=0, concat_axis=0, tiled=True
    )
    mine = own * 8 + jnp.arange(8)
    from_pair = jnp.any(stored[None, :, :] == mine[:, None, None], axis=2).astype(BF)
    from_pair = jnp.repeat(from_pair, 2, axis=1)
    total = jnp.dot(from_pair, back.reshape(128, 1024), preferred_element_type=F32)
    total = total.reshape(8, 4, 256)[:, :, :TOK]
    weight_total = total[:, 3]
    joined = total[:, :3] / jnp.maximum(weight_total, 1.0)[:, None, :]
    return (joined, weight_total)


def solution(mesh):
    placed = (
        P("img", None, "mdl"),
        P(),
        P(),
        P("img", None, None),
        P("img"),
        P(None, "mdl"),
        P(None, "mdl"),
        P(None, "mdl"),
        P("mdl", None),
        P("mdl", None),
        P(),
        P(),
    )
    return jax.shard_map(
        local,
        mesh=mesh,
        in_specs=placed,
        out_specs=(P("img", None, None), P("img", None)),
        check_vma=False,
    )
```

```python
import jax
import jax.numpy as jnp
from jax import lax
from jax.experimental import pallas as pl
from jax.experimental.pallas import tpu as pltpu
from jax.sharding import PartitionSpec as P

D = 1024
HALF = 512
HEAD_DIM = 64
TOK = 196
STEPS = 13
PAD_TOK = 208
ROWS = 2 * PAD_TOK
LANES = 128
AHEAD = 1
BF = jnp.bfloat16
F32 = jnp.float32
MIB = 1 << 20
HBM = pl.BlockSpec(memory_space=pltpu.HBM)
VMEM = pl.BlockSpec(memory_space=pltpu.VMEM)
SMEM = pl.BlockSpec(memory_space=pltpu.SMEM)


def iota(shape, axis):
    return lax.broadcasted_iota(jnp.int32, shape, axis)


def spread_kernel(pairs_ref, tokens_ref, out_ref, tokens, spread_rows, in_sem, out_sem):
    arrive, leave = [], []
    for half in range(2):
        lanes = slice(half * 256, half * 256 + 256)
        arrive.append(
            pltpu.make_async_copy(tokens_ref.at[:, :, lanes], tokens.at[half], in_sem.at[half])
        )
        leave.append(
            pltpu.make_async_copy(
                spread_rows.at[:, 2 * half : 2 * half + 2],
                out_ref.at[:, 2 * half : 2 * half + 2],
                out_sem.at[half],
            )
        )
        arrive[half].start()
    row, high = iota((8, LANES), 0), iota((8, LANES), 1) >= 64
    listed = jnp.zeros((8, LANES), F32)
    for entry in range(16):
        value = pairs_ref[entry % 2, entry // 2].astype(F32)
        place = (row == entry % 8) & (high if entry >= 8 else ~high)
        listed = jnp.where(place, value, listed)
    listed = jnp.broadcast_to(listed.astype(BF)[None, None], (16, 4, 8, LANES))
    spread_rows[:, :, :, STEPS * LANES :] = listed
    left = TOK - 16 * (STEPS - 1)
    spread_rows[left:, :, :, (STEPS - 1) * LANES : STEPS * LANES] = jnp.zeros((16 - left, 4, 8, LANES), BF)
    for half in range(2):
        arrive[half].wait()
        for step in range(STEPS):
            count = min(16, TOK - 16 * step)
            for group in range(2):
                spread_rows[:count, 2 * half + group, :, step * LANES : (step + 1) * LANES] = tokens[
                    half, 16 * step : 16 * step + count, :, group * LANES : (group + 1) * LANES
                ]
        leave[half].start()
    for half in range(2):
        leave[half].wait()


def in_hbm(*arrays):
    return [pltpu.with_memory_space_constraint(a, pltpu.HBM) for a in arrays]


def spread(pairs, tokens):
    shape = (16, 4, 8, 14 * LANES)
    return pl.pallas_call(
        spread_kernel,
        in_specs=[SMEM, HBM],
        out_specs=HBM,
        out_shape=pltpu.HBM(shape, BF),
        scratch_shapes=[
            pltpu.VMEM((2, TOK, 8, 256), BF),
            pltpu.VMEM(shape, BF),
            pltpu.SemaphoreType.DMA((2,)),
            pltpu.SemaphoreType.DMA((2,)),
        ],
        compiler_params=pltpu.CompilerParams(vmem_limit_bytes=24 * MIB),
    )(pairs, *in_hbm(tokens))


def select_kernel(pieces_ref, stored_ref, out_ref, chosen, sems):
    listed = pieces_ref[:, STEPS * LANES :].astype(F32).reshape(64, 8, LANES)
    lane = iota((64, 8, LANES), 2)
    image = jnp.where(listed == (lane & 63).astype(F32), stored_ref[...], 0.0)
    low = jnp.sum(jnp.where(lane < 64, image, 0.0), axis=2, keepdims=True)
    high = jnp.sum(jnp.where(lane < 64, 0.0, image), axis=2, keepdims=True)
    rows = jnp.concatenate([low[:, None], high[:, None]], axis=1).reshape(1024, 1)
    leave = []
    for part in range(4):
        mine = slice(part * 256, part * 256 + 256)
        hit = rows[mine] == iota((256, 512), 1).astype(F32)
        hit = jnp.where(hit, 1.0, 0.0).astype(BF)
        got = jnp.dot(hit, pieces_ref[:, : STEPS * LANES], preferred_element_type=F32)
        chosen[mine, :] = got.astype(BF)
        leave.append(pltpu.make_async_copy(chosen.at[mine], out_ref.at[mine], sems.at[part]))
        leave[part].start()
    for copy in leave:
        copy.wait()


def select(pieces, stored):
    shape = (1024, STEPS * LANES)
    return pl.pallas_call(
        select_kernel,
        in_specs=[VMEM, VMEM],
        out_specs=HBM,
        out_shape=pltpu.HBM(shape, BF),
        scratch_shapes=[pltpu.VMEM(shape, BF), pltpu.SemaphoreType.DMA((4,))],
        compiler_params=pltpu.CompilerParams(vmem_limit_bytes=24 * MIB),
    )(pieces, stored)


def pair_kernel(live_ref, owner_ref, pieces_ref, *refs):
    sources, out_ref = refs[:12], refs[12]
    weights = refs[13:25]
    x_ref, q_ref, k_ref, v_ref, att_ref, total_ref, send_ref, in_sem, out_sem = refs[25:]
    wo0, wo1, hin0, hin1, hmid, hlast = weights[6:]
    arrive = [
        pltpu.make_async_copy(source, weight, in_sem.at[i])
        for i, (source, weight) in enumerate(zip(sources, weights))
    ]
    for copy in arrive:
        copy.start()
    live = live_ref[0]

    out_row = iota((128, 128), 0)
    source = (out_row & 15) * 8 + (out_row >> 4)
    perm = jnp.where(source == iota((128, 128), 1), 1.0, 0.0).astype(BF)
    for step in range(STEPS):
        lanes = slice(step * LANES, (step + 1) * LANES)
        columns = []
        for core in range(2):
            for group in range(4):
                tile = pieces_ref[:, group, core, :, lanes].astype(F32)
                columns.append(tile.reshape(128, LANES).astype(BF))
        moved = jnp.dot(perm, jnp.concatenate(columns, axis=1), preferred_element_type=F32)
        x_ref[:, step * 16 : step * 16 + 16, :] = moved.astype(BF).reshape(8, 16, D)

    total_ref[...] = jnp.zeros_like(total_ref)

    def project(pair, first_use=False):
        x = x_ref[pl.ds(2 * pair, 2)].reshape(ROWS, D)
        for which in range(6):
            half, i = divmod(which, 3)
            cols = slice(half * HALF, (half + 1) * HALF)
            if first_use:
                arrive[which].wait()
            got = jnp.dot(x, weights[which][...], preferred_element_type=F32).astype(BF)
            if i == 0:
                got = got * jnp.asarray(HEAD_DIM**-0.5, BF)
            (q_ref, k_ref, v_ref)[i][:, cols] = got
            yield
        is_pad = iota((16, D), 0) >= TOK - 192
        for slot in range(2):
            tail = slice(slot * PAD_TOK + 192, (slot + 1) * PAD_TOK)
            key = k_ref[slot * PAD_TOK : slot * PAD_TOK + 16, :].astype(F32)[0:1]
            k_ref[tail, :] = jnp.where(is_pad, key, k_ref[tail, :].astype(F32)).astype(BF)

    def attend():
        first = iota((PAD_TOK, LANES), 1) < HEAD_DIM
        ones = jnp.where(iota((PAD_TOK, LANES), 0) < TOK, 1.0, 0.0).astype(BF)
        chains = [
            (
                slice(slot * PAD_TOK, (slot + 1) * PAD_TOK),
                slice((1 - slot) * PAD_TOK, (2 - slot) * PAD_TOK),
                slice(two * LANES, (two + 1) * LANES),
            )
            for two in range(D // LANES)
            for slot in range(2)
        ]
        scores = []
        for turn in range(len(chains) + AHEAD):
            if turn < len(chains):
                mine, other, cols = chains[turn]
                q = q_ref[mine, cols]
                none = jnp.zeros_like(q)
                both = jnp.concatenate([jnp.where(first, q, none), jnp.where(first, none, q)], axis=0)
                scores.append(
                    lax.dot_general(
                        both, k_ref[other, cols], (((1,), (1,)), ((), ())), preferred_element_type=F32
                    )
                )
            if turn >= AHEAD:
                mine, other, cols = chains[turn - AHEAD]
                score = scores[turn - AHEAD]
                weight = jnp.exp(score - jnp.max(score, axis=1, keepdims=True)).astype(BF)
                values = jnp.concatenate([v_ref[other, cols], ones], axis=1)
                got = jnp.dot(weight, values, preferred_element_type=F32)
                top = jnp.where(first, got[:PAD_TOK, :LANES], got[PAD_TOK:, :LANES])
                below = jnp.where(first, got[:PAD_TOK, LANES:], got[PAD_TOK:, LANES:])
                att_ref[mine, cols] = (top / below).astype(BF)

    def head(pair):
        x = x_ref[pl.ds(2 * pair, 2)].reshape(ROWS, D)
        mixed = x.astype(F32) + jnp.dot(att_ref[:, :HALF], wo0[...], preferred_element_type=F32)
        mixed = mixed + jnp.dot(att_ref[:, HALF:], wo1[...], preferred_element_type=F32)
        yield
        mean = jnp.sum(mixed, axis=1, keepdims=True) * (1.0 / D)
        square = jnp.sum(mixed * mixed, axis=1, keepdims=True) * (1.0 / D)
        normed = ((mixed - mean) * lax.rsqrt(square - mean * mean + 1e-05)).astype(BF)
        hidden = jnp.dot(normed[:, :HALF], hin0[...], preferred_element_type=F32)
        hidden = hidden + jnp.dot(normed[:, HALF:], hin1[...], preferred_element_type=F32)
        yield
        hidden = jax.nn.gelu(hidden).astype(BF)
        inner = jnp.dot(hidden, hmid[...], preferred_element_type=F32)
        yield
        inner = jax.nn.gelu(inner).astype(BF)
        for slot in range(2):
            last = lax.dot_general(
                hlast[...],
                inner[slot * PAD_TOK : (slot + 1) * PAD_TOK],
                (((1,), (1,)), ((), ())),
                preferred_element_type=F32,
            )
            logit = last[3:4, :]
            confidence = 1.0 + jnp.maximum(logit, 0.0) + jnp.log1p(jnp.exp(-jnp.abs(logit)))
            result = jnp.where(iota(last.shape, 0) == 3, 1.0, last) * confidence
            owner = owner_ref[2 * pair + slot]
            total_ref[owner, 0:4, :] += result[:, :LANES]
            total_ref[owner, 4:8, 0 : PAD_TOK - LANES] += result[:, LANES:]

    def run(*stages):
        stages = list(stages)
        while stages:
            stages = [stage for stage in stages if next(stage, stages) is None]

    run(project(0, first_use=True))
    attend()
    for copy in arrive[6:]:
        copy.wait()

    def step(pair, carry):
        run(head(pair - 1), project(pair))
        attend()
        return carry

    lax.fori_loop(1, live, step, 0)

    @pl.when(live > 0)
    def _():
        run(head(live - 1))

    send_ref[...] = total_ref[...].astype(BF)
    leave = [pltpu.make_async_copy(send_ref, out_ref.at[:, to], out_sem.at[to]) for to in range(2)]
    for copy in leave:
        copy.start()
    for copy in leave:
        copy.wait()


def pair_heads(live, owners, pieces, weights):
    send = (64, 2, 8, LANES)
    return pl.pallas_call(
        pair_kernel,
        in_specs=[SMEM, SMEM, VMEM] + [HBM] * len(weights),
        out_specs=HBM,
        out_shape=pltpu.HBM(send, BF),
        scratch_shapes=[pltpu.VMEM(a.shape, BF) for a in weights]
        + [pltpu.VMEM((8, PAD_TOK, D), BF)]
        + [pltpu.VMEM((ROWS, D), BF)] * 4
        + [
            pltpu.VMEM((64, 8, LANES), F32),
            pltpu.VMEM((64, 8, LANES), BF),
            pltpu.SemaphoreType.DMA((len(weights),)),
            pltpu.SemaphoreType.DMA((2,)),
        ],
        compiler_params=pltpu.CompilerParams(vmem_limit_bytes=44 * MIB),
    )(live, owners, pieces, *in_hbm(*weights))


def join_kernel(place_ref, back_ref, joined_ref, weight_ref):
    total = jnp.dot(place_ref[...], back_ref[...], preferred_element_type=F32).reshape(8, 8, LANES)
    for start, lanes in ((0, LANES), (4, TOK - LANES)):
        weight = total[start + 3, :, :lanes]
        cols = slice(start * 32, start * 32 + lanes)
        below = jnp.maximum(weight, 1.0)
        for axis in range(3):
            joined_ref[axis, :, cols] = total[start + axis, :, :lanes] / below
        weight_ref[:, cols] = weight


def join(place, back):
    return pl.pallas_call(
        join_kernel,
        in_specs=[VMEM, VMEM],
        out_specs=(VMEM, VMEM),
        out_shape=(
            jax.ShapeDtypeStruct((3, 8, TOK), F32),
            jax.ShapeDtypeStruct((8, TOK), F32),
        ),
        compiler_params=pltpu.CompilerParams(vmem_limit_bytes=8 * MIB),
    )(place, back)


def local(
    tokens,
    image_row,
    views,
    pairs,
    pair_count,
    w_query,
    w_key,
    w_value,
    w_out,
    head_in,
    head_mid,
    head_last,
):
    own = lax.axis_index("img")
    core = lax.axis_index("mdl")

    outgoing = spread(pairs[0].T, tokens.transpose(1, 0, 2)).reshape(64, 8, 14 * LANES)
    pieces = lax.all_to_all(outgoing, "img", split_axis=0, concat_axis=0, tiled=True)

    swap = lambda a: lax.ppermute(a, "mdl", [(0, 1), (1, 0)])
    q_other, k_other, v_other, o_other, h_other = (
        swap(a) for a in (w_query, w_key, w_value, w_out, head_in)
    )
    low = core == 0
    hin0 = jnp.where(low, head_in, h_other)
    hin1 = jnp.where(low, h_other, head_in)

    is_image = views[:, :, None] == jnp.arange(image_row.shape[0])
    stored = jnp.sum(jnp.where(is_image, image_row, 0), axis=2)
    stored_lanes = jnp.pad(stored.astype(F32), ((0, 0), (0, 48)))
    stored_lanes = jnp.concatenate([stored_lanes, stored_lanes], axis=1).reshape(64, 1, LANES)

    chosen = select(pieces.reshape(512, 14 * LANES), stored_lanes)
    arrived = lax.all_to_all(
        chosen.reshape(128, 8, STEPS * LANES),
        ("img", "mdl"),
        split_axis=0,
        concat_axis=0,
        tiled=True,
    )

    my_stored = lax.dynamic_index_in_dim(stored, own, 0, keepdims=False)
    my_views = lax.dynamic_slice_in_dim(pairs.reshape(16), 8 * core, 8, 0)
    my_rows = jnp.sum(jnp.where(my_views[:, None] == jnp.arange(16), my_stored, 0), axis=1)
    live = jnp.clip(pair_count - 4 * core, 0, 4)
    sums = pair_heads(
        live,
        my_rows // 8,
        arrived.reshape(16, 4, 2, 8, STEPS * LANES),
        (w_query, w_key, w_value, q_other, k_other, v_other, w_out, o_other, hin0, hin1, head_mid, head_last),
    )

    back = lax.all_to_all(
        sums.reshape(128, 8, LANES), ("img", "mdl"), split_axis=0, concat_axis=0, tiled=True
    )
    mine = own * 8 + jnp.arange(8)
    named = jnp.any(stored[None, :, :] == mine[:, None, None], axis=2)
    place = jnp.eye(8, dtype=bool)[:, None, None, None, :] & named[None, :, :, None, None]
    place = jnp.broadcast_to(place, (8, 8, 64, 2, 8)).astype(BF).reshape(64, 1024)
    joined, weight_total = join(place, back.reshape(1024, LANES))
    return (joined.transpose(1, 0, 2), weight_total)


def solution(mesh):
    placed = (
        P("img", None, "mdl"),
        P(),
        P(),
        P("img", None, None),
        P("img"),
        P(None, "mdl"),
        P(None, "mdl"),
        P(None, "mdl"),
        P("mdl", None),
        P("mdl", None),
        P(),
        P(),
    )
    return jax.shard_map(
        local,
        mesh=mesh,
        in_specs=placed,
        out_specs=(P("img", None, None), P("img", None)),
        check_vma=False,
    )
```

```python
import jax
import jax.numpy as jnp
from jax import lax
from jax.experimental import pallas as pl
from jax.experimental.pallas import tpu as pltpu
from jax.sharding import PartitionSpec as P

D = 1024
HALF = 512
HEAD_DIM = 64
TOK = 196
STEPS = 13
PAD_TOK = 208
ROWS = 2 * PAD_TOK
LANES = 128
AHEAD = 1
SELECT_PARTS = ((0, 384), (384, 704), (704, 896), (896, 1024))
FIRST = 3
DEPTH = 4
SPREAD_PARTS = tuple((low, low + 2) for low in range(0, 14, 2))
BF = jnp.bfloat16
F32 = jnp.float32
MIB = 1 << 20
HBM = pl.BlockSpec(memory_space=pltpu.HBM)
VMEM = pl.BlockSpec(memory_space=pltpu.VMEM)
SMEM = pl.BlockSpec(memory_space=pltpu.SMEM)


def iota(shape, axis):
    return lax.broadcasted_iota(jnp.int32, shape, axis)


def spread_kernel(pairs_ref, tokens_ref, out_ref, pairs, tokens, spread_rows, pairs_sem, in_sem, out_sem):
    get_pairs = pltpu.make_async_copy(pairs_ref, pairs, pairs_sem)
    arrive, leave = [], []
    for part, (low, high) in enumerate(SPREAD_PARTS):
        mine = slice(16 * low, min(16 * high, TOK))
        arrive.append(pltpu.make_async_copy(tokens_ref.at[mine], tokens.at[mine], in_sem.at[part]))
        lanes = slice(low * LANES, high * LANES)
        leave.append(
            pltpu.make_async_copy(
                spread_rows.at[:, :, :, lanes], out_ref.at[:, :, :, lanes], out_sem.at[part]
            )
        )
        arrive[part].start()
    get_pairs.start()
    for part, (low, high) in enumerate(SPREAD_PARTS):
        arrive[part].wait()
        for step in range(low, min(high, STEPS)):
            count = min(16, TOK - 16 * step)
            lanes = slice(step * LANES, (step + 1) * LANES)
            for group in range(4):
                spread_rows[:count, group, :, lanes] = tokens[
                    16 * step : 16 * step + count, :, group * LANES : (group + 1) * LANES
                ]
            if count < 16:
                spread_rows[count:, :, :, lanes] = jnp.zeros((16 - count, 4, 8, LANES), BF)
        if high > STEPS:
            get_pairs.wait()
            row, upper = iota((8, LANES), 0), iota((8, LANES), 1) >= 64
            listed = jnp.zeros((8, LANES), F32)
            for entry in range(16):
                value = pairs[entry % 2, entry // 2].astype(F32)
                place = (row == entry % 8) & (upper if entry >= 8 else ~upper)
                listed = jnp.where(place, value, listed)
            spread_rows[:, :, :, STEPS * LANES :] = jnp.broadcast_to(
                listed.astype(BF)[None, None], (16, 4, 8, LANES)
            )
        leave[part].start()
    for copy in leave:
        copy.wait()


def in_hbm(*arrays):
    return [pltpu.with_memory_space_constraint(a, pltpu.HBM) for a in arrays]


def spread(pairs, tokens):
    shape = (16, 4, 8, 14 * LANES)
    return pl.pallas_call(
        spread_kernel,
        in_specs=[HBM, HBM],
        out_specs=HBM,
        out_shape=pltpu.HBM(shape, BF),
        scratch_shapes=[
            pltpu.SMEM((2, 8), jnp.int32),
            pltpu.VMEM((TOK, 8, HALF), BF),
            pltpu.VMEM(shape, BF),
            pltpu.SemaphoreType.DMA,
            pltpu.SemaphoreType.DMA((len(SPREAD_PARTS),)),
            pltpu.SemaphoreType.DMA((len(SPREAD_PARTS),)),
        ],
        compiler_params=pltpu.CompilerParams(vmem_limit_bytes=24 * MIB),
    )(*in_hbm(pairs, tokens))


def select_kernel(pieces_ref, stored_ref, out_ref, chosen, sems):
    listed = pieces_ref[:, STEPS * LANES :].astype(F32).reshape(64, 8, LANES)
    lane = iota((64, 8, LANES), 2)
    image = jnp.where(listed == (lane & 63).astype(F32), stored_ref[...], 0.0)
    low = jnp.sum(jnp.where(lane < 64, image, 0.0), axis=2, keepdims=True)
    high = jnp.sum(jnp.where(lane < 64, 0.0, image), axis=2, keepdims=True)
    rows = jnp.concatenate([low[:, None], high[:, None]], axis=1).reshape(1024, 1)
    leave = []
    for part, (begin, end) in enumerate(SELECT_PARTS):
        mine = slice(begin, end)
        hit = rows[mine] == iota((end - begin, 512), 1).astype(F32)
        hit = jnp.where(hit, 1.0, 0.0).astype(BF)
        got = jnp.dot(hit, pieces_ref[:, : STEPS * LANES], preferred_element_type=F32)
        chosen[mine, :] = got.astype(BF)
        leave.append(pltpu.make_async_copy(chosen.at[mine], out_ref.at[mine], sems.at[part]))
        leave[part].start()
    for copy in leave:
        copy.wait()


def select(pieces, stored):
    shape = (1024, STEPS * LANES)
    return pl.pallas_call(
        select_kernel,
        in_specs=[VMEM, VMEM],
        out_specs=HBM,
        out_shape=pltpu.HBM(shape, BF),
        scratch_shapes=[pltpu.VMEM(shape, BF), pltpu.SemaphoreType.DMA((len(SELECT_PARTS),))],
        compiler_params=pltpu.CompilerParams(vmem_limit_bytes=24 * MIB),
    )(pieces, stored)


def pair_kernel(live_ref, owner_ref, pieces_ref, *refs):
    sources, out_ref = refs[:12], refs[12]
    weights = refs[13:25]
    x_ref, q_ref, k_ref, v_ref, att_ref, total_ref, send_ref, in_sem, out_sem = refs[25:]
    wo0, wo1, hin0, hin1, hmid, hlast = weights[6:]
    arrive = [
        pltpu.make_async_copy(source, weight, in_sem.at[i])
        for i, (source, weight) in enumerate(zip(sources, weights))
    ]
    for copy in arrive[:FIRST]:
        copy.start()
    live = live_ref[0]

    out_row = iota((128, 128), 0)
    source = (out_row & 15) * 8 + (out_row >> 4)
    perm = jnp.where(source == iota((128, 128), 1), 1.0, 0.0).astype(BF)
    for step in range(STEPS):
        if step == STEPS // 2:
            for copy in arrive[FIRST:DEPTH]:
                copy.start()
        lanes = slice(step * LANES, (step + 1) * LANES)
        columns = []
        for core in range(2):
            for group in range(4):
                tile = pieces_ref[:, group, core, :, lanes].astype(F32)
                columns.append(tile.reshape(128, LANES).astype(BF))
        moved = jnp.dot(perm, jnp.concatenate(columns, axis=1), preferred_element_type=F32)
        x_ref[:, step * 16 : step * 16 + 16, :] = moved.astype(BF).reshape(8, 16, D)

    total_ref[...] = jnp.zeros_like(total_ref)

    def project(pair, first_use=False):
        x = x_ref[pl.ds(2 * pair, 2)].reshape(ROWS, D)
        for which in range(6):
            half, i = divmod(which, 3)
            cols = slice(half * HALF, (half + 1) * HALF)
            if first_use:
                arrive[which].wait()
                for copy in arrive[DEPTH + 2 * which : DEPTH + 2 * which + 2]:
                    copy.start()
            got = jnp.dot(x, weights[which][...], preferred_element_type=F32).astype(BF)
            if i == 0:
                got = got * jnp.asarray(HEAD_DIM**-0.5, BF)
            (q_ref, k_ref, v_ref)[i][:, cols] = got
            yield
        is_pad = iota((16, D), 0) >= TOK - 192
        for slot in range(2):
            tail = slice(slot * PAD_TOK + 192, (slot + 1) * PAD_TOK)
            key = k_ref[slot * PAD_TOK : slot * PAD_TOK + 16, :].astype(F32)[0:1]
            k_ref[tail, :] = jnp.where(is_pad, key, k_ref[tail, :].astype(F32)).astype(BF)

    def attend():
        first = iota((PAD_TOK, LANES), 1) < HEAD_DIM
        ones = jnp.where(iota((PAD_TOK, LANES), 0) < TOK, 1.0, 0.0).astype(BF)
        chains = [
            (
                slice(slot * PAD_TOK, (slot + 1) * PAD_TOK),
                slice((1 - slot) * PAD_TOK, (2 - slot) * PAD_TOK),
                slice(two * LANES, (two + 1) * LANES),
            )
            for two in range(D // LANES)
            for slot in range(2)
        ]
        scores = []
        for turn in range(len(chains) + AHEAD):
            if turn < len(chains):
                mine, other, cols = chains[turn]
                q = q_ref[mine, cols]
                none = jnp.zeros_like(q)
                both = jnp.concatenate([jnp.where(first, q, none), jnp.where(first, none, q)], axis=0)
                scores.append(
                    lax.dot_general(
                        both, k_ref[other, cols], (((1,), (1,)), ((), ())), preferred_element_type=F32
                    )
                )
            if turn >= AHEAD:
                mine, other, cols = chains[turn - AHEAD]
                score = scores[turn - AHEAD]
                weight = jnp.exp(score - jnp.max(score, axis=1, keepdims=True)).astype(BF)
                values = jnp.concatenate([v_ref[other, cols], ones], axis=1)
                got = jnp.dot(weight, values, preferred_element_type=F32)
                top = jnp.where(first, got[:PAD_TOK, :LANES], got[PAD_TOK:, :LANES])
                below = jnp.where(first, got[:PAD_TOK, LANES:], got[PAD_TOK:, LANES:])
                att_ref[mine, cols] = (top / below).astype(BF)

    def head(pair):
        x = x_ref[pl.ds(2 * pair, 2)].reshape(ROWS, D)
        mixed = x.astype(F32) + jnp.dot(att_ref[:, :HALF], wo0[...], preferred_element_type=F32)
        mixed = mixed + jnp.dot(att_ref[:, HALF:], wo1[...], preferred_element_type=F32)
        yield
        mean = jnp.sum(mixed, axis=1, keepdims=True) * (1.0 / D)
        square = jnp.sum(mixed * mixed, axis=1, keepdims=True) * (1.0 / D)
        normed = ((mixed - mean) * lax.rsqrt(square - mean * mean + 1e-05)).astype(BF)
        hidden = jnp.dot(normed[:, :HALF], hin0[...], preferred_element_type=F32)
        hidden = hidden + jnp.dot(normed[:, HALF:], hin1[...], preferred_element_type=F32)
        yield
        hidden = jax.nn.gelu(hidden).astype(BF)
        inner = jnp.dot(hidden, hmid[...], preferred_element_type=F32)
        yield
        inner = jax.nn.gelu(inner).astype(BF)
        for slot in range(2):
            last = lax.dot_general(
                hlast[...],
                inner[slot * PAD_TOK : (slot + 1) * PAD_TOK],
                (((1,), (1,)), ((), ())),
                preferred_element_type=F32,
            )
            logit = last[3:4, :]
            confidence = 1.0 + jnp.maximum(logit, 0.0) + jnp.log1p(jnp.exp(-jnp.abs(logit)))
            result = jnp.where(iota(last.shape, 0) == 3, 1.0, last) * confidence
            owner = owner_ref[2 * pair + slot]
            total_ref[owner, 0:4, :] += result[:, :LANES]
            total_ref[owner, 4:8, 0 : PAD_TOK - LANES] += result[:, LANES:]

    def run(*stages):
        stages = list(stages)
        while stages:
            stages = [stage for stage in stages if next(stage, stages) is None]

    run(project(0, first_use=True))
    attend()
    for copy in arrive[6:]:
        copy.wait()

    def step(pair, carry):
        run(head(pair - 1), project(pair))
        attend()
        return carry

    lax.fori_loop(1, live, step, 0)

    @pl.when(live > 0)
    def _():
        run(head(live - 1))

    send_ref[...] = total_ref[...].astype(BF)
    leave = [pltpu.make_async_copy(send_ref, out_ref.at[:, to], out_sem.at[to]) for to in range(2)]
    for copy in leave:
        copy.start()
    for copy in leave:
        copy.wait()


def pair_heads(live, owners, pieces, weights):
    send = (64, 2, 8, LANES)
    return pl.pallas_call(
        pair_kernel,
        in_specs=[SMEM, SMEM, VMEM] + [HBM] * len(weights),
        out_specs=HBM,
        out_shape=pltpu.HBM(send, BF),
        scratch_shapes=[pltpu.VMEM(a.shape, BF) for a in weights]
        + [pltpu.VMEM((8, PAD_TOK, D), BF)]
        + [pltpu.VMEM((ROWS, D), BF)] * 4
        + [
            pltpu.VMEM((64, 8, LANES), F32),
            pltpu.VMEM((64, 8, LANES), BF),
            pltpu.SemaphoreType.DMA((len(weights),)),
            pltpu.SemaphoreType.DMA((2,)),
        ],
        compiler_params=pltpu.CompilerParams(vmem_limit_bytes=44 * MIB),
    )(live, owners, pieces, *in_hbm(*weights))


def join_kernel(place_ref, back_ref, joined_ref, weight_ref):
    total = jnp.dot(place_ref[...], back_ref[...], preferred_element_type=F32).reshape(8, 8, LANES)
    for start, lanes in ((0, LANES), (4, TOK - LANES)):
        weight = total[start + 3, :, :lanes]
        cols = slice(start * 32, start * 32 + lanes)
        below = jnp.maximum(weight, 1.0)
        for axis in range(3):
            joined_ref[axis, :, cols] = total[start + axis, :, :lanes] / below
        weight_ref[:, cols] = weight


def join(place, back):
    return pl.pallas_call(
        join_kernel,
        in_specs=[VMEM, VMEM],
        out_specs=(VMEM, VMEM),
        out_shape=(
            jax.ShapeDtypeStruct((3, 8, TOK), F32),
            jax.ShapeDtypeStruct((8, TOK), F32),
        ),
        compiler_params=pltpu.CompilerParams(vmem_limit_bytes=8 * MIB),
    )(place, back)


def local(
    tokens,
    image_row,
    views,
    pairs,
    pair_count,
    w_query,
    w_key,
    w_value,
    w_out,
    head_in,
    head_mid,
    head_last,
):
    own = lax.axis_index("img")
    core = lax.axis_index("mdl")

    outgoing = spread(pairs[0].T, tokens.transpose(1, 0, 2)).reshape(64, 8, 14 * LANES)
    pieces = lax.all_to_all(outgoing, "img", split_axis=0, concat_axis=0, tiled=True)

    swap = lambda a: lax.ppermute(a, "mdl", [(0, 1), (1, 0)])
    q_other, k_other, v_other, o_other, h_other = (
        swap(a) for a in (w_query, w_key, w_value, w_out, head_in)
    )
    low = core == 0
    hin0 = jnp.where(low, head_in, h_other)
    hin1 = jnp.where(low, h_other, head_in)

    is_image = views[:, :, None] == jnp.arange(image_row.shape[0])
    stored = jnp.sum(jnp.where(is_image, image_row, 0), axis=2)
    stored_lanes = jnp.pad(stored.astype(F32), ((0, 0), (0, 48)))
    stored_lanes = jnp.concatenate([stored_lanes, stored_lanes], axis=1).reshape(64, 1, LANES)

    chosen = select(pieces.reshape(512, 14 * LANES), stored_lanes)
    arrived = lax.all_to_all(
        chosen.reshape(128, 8, STEPS * LANES),
        ("img", "mdl"),
        split_axis=0,
        concat_axis=0,
        tiled=True,
    )

    my_stored = lax.dynamic_index_in_dim(stored, own, 0, keepdims=False)
    my_views = lax.dynamic_slice_in_dim(pairs.reshape(16), 8 * core, 8, 0)
    my_rows = jnp.sum(jnp.where(my_views[:, None] == jnp.arange(16), my_stored, 0), axis=1)
    live = jnp.clip(pair_count - 4 * core, 0, 4)
    sums = pair_heads(
        live,
        my_rows // 8,
        arrived.reshape(16, 4, 2, 8, STEPS * LANES),
        (w_query, w_key, w_value, q_other, k_other, v_other, w_out, o_other, hin0, hin1, head_mid, head_last),
    )

    back = lax.all_to_all(
        sums.reshape(128, 8, LANES), ("img", "mdl"), split_axis=0, concat_axis=0, tiled=True
    )
    mine = own * 8 + jnp.arange(8)
    named = jnp.any(stored[None, :, :] == mine[:, None, None], axis=2)
    place = jnp.eye(8, dtype=bool)[:, None, None, None, :] & named[None, :, :, None, None]
    place = jnp.broadcast_to(place, (8, 8, 64, 2, 8)).astype(BF).reshape(64, 1024)
    joined, weight_total = join(place, back.reshape(1024, LANES))
    return (joined.transpose(1, 0, 2), weight_total)


def solution(mesh):
    placed = (
        P("img", None, "mdl"),
        P(),
        P(),
        P("img", None, None),
        P("img"),
        P(None, "mdl"),
        P(None, "mdl"),
        P(None, "mdl"),
        P("mdl", None),
        P("mdl", None),
        P(),
        P(),
    )
    return jax.shard_map(
        local,
        mesh=mesh,
        in_specs=placed,
        out_specs=(P("img", None, None), P("img", None)),
        check_vma=False,
    )
```

```python
import jax
import jax.numpy as jnp
from jax import lax
from jax.experimental import pallas as pl
from jax.experimental.pallas import tpu as pltpu
from jax.sharding import PartitionSpec as P

D = 1024
HALF = 512
HEAD_DIM = 64
TOK = 196
STEPS = 13
PAD_TOK = 208
ROWS = 2 * PAD_TOK
LANES = 128
AHEAD = 1
WAITS = {0: (0, 1), 1: (1, 3), 3: (3, 6)}
SELECT_PARTS = ((0, 384), (384, 704), (704, 896), (896, 1024))
SPREAD_PARTS = tuple((low, low + 2) for low in range(0, 14, 2))
BF = jnp.bfloat16
F32 = jnp.float32
MIB = 1 << 20
HBM = pl.BlockSpec(memory_space=pltpu.HBM)
VMEM = pl.BlockSpec(memory_space=pltpu.VMEM)
SMEM = pl.BlockSpec(memory_space=pltpu.SMEM)


def iota(shape, axis):
    return lax.broadcasted_iota(jnp.int32, shape, axis)


def spread_kernel(pairs_ref, tokens_ref, out_ref, pairs, tokens, spread_rows, pairs_sem, in_sem, out_sem):
    get_pairs = pltpu.make_async_copy(pairs_ref, pairs, pairs_sem)
    arrive, leave = [], []
    for part, (low, high) in enumerate(SPREAD_PARTS):
        mine = slice(16 * low, min(16 * high, TOK))
        arrive.append(pltpu.make_async_copy(tokens_ref.at[mine], tokens.at[mine], in_sem.at[part]))
        lanes = slice(low * LANES, high * LANES)
        leave.append(
            pltpu.make_async_copy(
                spread_rows.at[:, :, :, lanes], out_ref.at[:, :, :, lanes], out_sem.at[part]
            )
        )
        arrive[part].start()
    get_pairs.start()
    for part, (low, high) in enumerate(SPREAD_PARTS):
        arrive[part].wait()
        for step in range(low, min(high, STEPS)):
            count = min(16, TOK - 16 * step)
            lanes = slice(step * LANES, (step + 1) * LANES)
            for group in range(4):
                spread_rows[:count, group, :, lanes] = tokens[
                    16 * step : 16 * step + count, :, group * LANES : (group + 1) * LANES
                ]
            if count < 16:
                spread_rows[count:, :, :, lanes] = jnp.zeros((16 - count, 4, 8, LANES), BF)
        if high > STEPS:
            get_pairs.wait()
            row, upper = iota((8, LANES), 0), iota((8, LANES), 1) >= 64
            listed = jnp.zeros((8, LANES), F32)
            for entry in range(16):
                value = pairs[entry % 2, entry // 2].astype(F32)
                place = (row == entry % 8) & (upper if entry >= 8 else ~upper)
                listed = jnp.where(place, value, listed)
            spread_rows[:, :, :, STEPS * LANES :] = jnp.broadcast_to(
                listed.astype(BF)[None, None], (16, 4, 8, LANES)
            )
        leave[part].start()
    for copy in leave:
        copy.wait()


def in_hbm(*arrays):
    return [pltpu.with_memory_space_constraint(a, pltpu.HBM) for a in arrays]


def spread(pairs, tokens):
    shape = (16, 4, 8, 14 * LANES)
    return pl.pallas_call(
        spread_kernel,
        in_specs=[HBM, HBM],
        out_specs=HBM,
        out_shape=pltpu.HBM(shape, BF),
        scratch_shapes=[
            pltpu.SMEM((2, 8), jnp.int32),
            pltpu.VMEM((TOK, 8, HALF), BF),
            pltpu.VMEM(shape, BF),
            pltpu.SemaphoreType.DMA,
            pltpu.SemaphoreType.DMA((len(SPREAD_PARTS),)),
            pltpu.SemaphoreType.DMA((len(SPREAD_PARTS),)),
        ],
        compiler_params=pltpu.CompilerParams(vmem_limit_bytes=24 * MIB),
    )(*in_hbm(pairs, tokens))


def select_kernel(pieces_ref, stored_ref, out_ref, chosen, sems):
    listed = pieces_ref[:, STEPS * LANES :].astype(F32).reshape(64, 8, LANES)
    lane = iota((64, 8, LANES), 2)
    image = jnp.where(listed == (lane & 63).astype(F32), stored_ref[...], 0.0)
    low = jnp.sum(jnp.where(lane < 64, image, 0.0), axis=2, keepdims=True)
    high = jnp.sum(jnp.where(lane < 64, 0.0, image), axis=2, keepdims=True)
    rows = jnp.concatenate([low[:, None], high[:, None]], axis=1).reshape(1024, 1)
    leave = []
    for part, (begin, end) in enumerate(SELECT_PARTS):
        mine = slice(begin, end)
        hit = rows[mine] == iota((end - begin, 512), 1).astype(F32)
        hit = jnp.where(hit, 1.0, 0.0).astype(BF)
        got = jnp.dot(hit, pieces_ref[:, : STEPS * LANES], preferred_element_type=F32)
        chosen[mine, :] = got.astype(BF)
        leave.append(pltpu.make_async_copy(chosen.at[mine], out_ref.at[mine], sems.at[part]))
        leave[part].start()
    for copy in leave:
        copy.wait()


def select(pieces, stored):
    shape = (1024, STEPS * LANES)
    return pl.pallas_call(
        select_kernel,
        in_specs=[VMEM, VMEM],
        out_specs=HBM,
        out_shape=pltpu.HBM(shape, BF),
        scratch_shapes=[pltpu.VMEM(shape, BF), pltpu.SemaphoreType.DMA((len(SELECT_PARTS),))],
        compiler_params=pltpu.CompilerParams(vmem_limit_bytes=24 * MIB),
    )(pieces, stored)


def pair_kernel(owner_ref, pieces_ref, *refs):
    sources, out_ref = refs[:12], refs[12]
    weights = refs[13:25]
    x_ref, q_ref, k_ref, v_ref, att_ref, total_ref, send_ref, in_sem, out_sem = refs[25:]
    wo0, wo1, hin0, hin1, hmid, hlast = weights[6:]
    arrive = [
        pltpu.make_async_copy(source, weight, in_sem.at[i])
        for i, (source, weight) in enumerate(zip(sources, weights))
    ]
    for copy in arrive[:6]:
        copy.start()

    out_row = iota((128, 128), 0)
    source = (out_row & 15) * 8 + (out_row >> 4)
    perm = jnp.where(source == iota((128, 128), 1), 1.0, 0.0).astype(BF)
    for step in range(STEPS):
        lanes = slice(step * LANES, (step + 1) * LANES)
        columns = []
        for core in range(2):
            for group in range(4):
                tile = pieces_ref[:, group, core, :, lanes].astype(F32)
                columns.append(tile.reshape(128, LANES).astype(BF))
        moved = jnp.dot(perm, jnp.concatenate(columns, axis=1), preferred_element_type=F32)
        x_ref[:, step * 16 : step * 16 + 16, :] = moved.astype(BF).reshape(8, 16, D)

    total_ref[...] = jnp.zeros_like(total_ref)

    def project(duo, begin=0, end=6):
        x = x_ref[4 * duo : 4 * duo + 4].reshape(2 * ROWS, D)
        for which in range(begin, end):
            half, i = divmod(which, 3)
            cols = slice(half * HALF, (half + 1) * HALF)
            if duo == 0 and which in WAITS:
                for copy in arrive[slice(*WAITS[which])]:
                    copy.wait()
                if which == 1:
                    for copy in arrive[6:]:
                        copy.start()
            got = jnp.dot(x, weights[which][...], preferred_element_type=F32).astype(BF)
            if i == 0:
                got = got * jnp.asarray(HEAD_DIM**-0.5, BF)
            (q_ref, k_ref, v_ref)[i][duo, :, cols] = got
            if i == 1:
                is_pad = iota((16, HALF), 0) >= TOK - 192
                for slot in range(4):
                    start = slot * PAD_TOK
                    tail = slice(start + 192, start + PAD_TOK)
                    key = k_ref[duo, start : start + 16, cols].astype(F32)[0:1]
                    keys = jnp.where(is_pad, key, k_ref[duo, tail, cols].astype(F32))
                    k_ref[duo, tail, cols] = keys.astype(BF)
            yield

    def attend(*pairs):
        first = iota((PAD_TOK, LANES), 1) < HEAD_DIM
        ones = jnp.where(iota((PAD_TOK, LANES), 0) < TOK, 1.0, 0.0).astype(BF)
        block = lambda slot: slice(slot * PAD_TOK, (slot + 1) * PAD_TOK)
        chains = [
            (
                pair // 2,
                block(2 * (pair % 2) + slot),
                block(2 * (pair % 2) + 1 - slot),
                slice(two * LANES, (two + 1) * LANES),
            )
            for pair in pairs
            for two in range(D // LANES)
            for slot in range(2)
        ]
        scores = []
        for turn in range(len(chains) + AHEAD):
            if turn < len(chains):
                duo, mine, other, cols = chains[turn]
                q = q_ref[duo, mine, cols]
                none = jnp.zeros_like(q)
                both = jnp.concatenate([jnp.where(first, q, none), jnp.where(first, none, q)], axis=0)
                scores.append(
                    lax.dot_general(
                        both, k_ref[duo, other, cols], (((1,), (1,)), ((), ())), preferred_element_type=F32
                    )
                )
            if turn >= AHEAD:
                duo, mine, other, cols = chains[turn - AHEAD]
                score = scores[turn - AHEAD]
                weight = jnp.exp(score - jnp.max(score, axis=1, keepdims=True)).astype(BF)
                values = jnp.concatenate([v_ref[duo, other, cols], ones], axis=1)
                got = jnp.dot(weight, values, preferred_element_type=F32)
                top = jnp.where(first, got[:PAD_TOK, :LANES], got[PAD_TOK:, :LANES])
                below = jnp.where(first, got[:PAD_TOK, LANES:], got[PAD_TOK:, LANES:])
                att_ref[duo, mine, cols] = (top / below).astype(BF)

    def head(*pairs):
        count = 2 * len(pairs)
        x = x_ref[2 * pairs[0] : 2 * pairs[0] + count].reshape(count * PAD_TOK, D)
        start = 2 * (pairs[0] % 2) * PAD_TOK
        att = att_ref.at[pairs[0] // 2, start : start + count * PAD_TOK]
        mixed = x.astype(F32) + jnp.dot(att[:, :HALF], wo0[...], preferred_element_type=F32)
        mixed = mixed + jnp.dot(att[:, HALF:], wo1[...], preferred_element_type=F32)
        yield
        mean = jnp.sum(mixed, axis=1, keepdims=True) * (1.0 / D)
        square = jnp.sum(mixed * mixed, axis=1, keepdims=True) * (1.0 / D)
        normed = ((mixed - mean) * lax.rsqrt(square - mean * mean + 1e-05)).astype(BF)
        hidden = jnp.dot(normed[:, :HALF], hin0[...], preferred_element_type=F32)
        hidden = hidden + jnp.dot(normed[:, HALF:], hin1[...], preferred_element_type=F32)
        yield
        hidden = jax.nn.gelu(hidden).astype(BF)
        inner = jnp.dot(hidden, hmid[...], preferred_element_type=F32)
        yield
        inner = jax.nn.gelu(inner).astype(BF)
        for slot in range(count):
            last = lax.dot_general(
                hlast[...],
                inner[slot * PAD_TOK : (slot + 1) * PAD_TOK],
                (((1,), (1,)), ((), ())),
                preferred_element_type=F32,
            )
            logit = last[3:4, :]
            confidence = 1.0 + jnp.maximum(logit, 0.0) + jnp.log1p(jnp.exp(-jnp.abs(logit)))
            result = jnp.where(iota(last.shape, 0) == 3, 1.0, last) * confidence
            owner = owner_ref[2 * pairs[0] + slot]
            total_ref[owner, 0:4, :] += result[:, :LANES]
            total_ref[owner, 4:8, 0 : PAD_TOK - LANES] += result[:, LANES:]

    def run(*stages):
        stages = list(stages)
        while stages:
            stages = [stage for stage in stages if next(stage, stages) is None]

    run(project(0))
    attend(0)
    for copy in arrive[6:]:
        copy.wait()
    run(head(0), project(1, 0, 3))
    attend(1)
    run(head(1), project(1, 3, 6))
    attend(2, 3)
    run(head(2, 3))
    send_ref[...] = total_ref[0:64].astype(BF)
    leave = [pltpu.make_async_copy(send_ref, out_ref.at[:, to], out_sem.at[to]) for to in range(2)]
    for copy in leave:
        copy.start()
    for copy in leave:
        copy.wait()


def pair_heads(owners, pieces, weights):
    send = (64, 2, 8, LANES)
    return pl.pallas_call(
        pair_kernel,
        in_specs=[SMEM, VMEM] + [HBM] * len(weights),
        out_specs=HBM,
        out_shape=pltpu.HBM(send, BF),
        scratch_shapes=[pltpu.VMEM(a.shape, BF) for a in weights]
        + [pltpu.VMEM((8, PAD_TOK, D), BF)]
        + [pltpu.VMEM((2, 2 * ROWS, D), BF)] * 4
        + [
            pltpu.VMEM((65, 8, LANES), F32),
            pltpu.VMEM((64, 8, LANES), BF),
            pltpu.SemaphoreType.DMA((len(weights),)),
            pltpu.SemaphoreType.DMA((2,)),
        ],
        compiler_params=pltpu.CompilerParams(vmem_limit_bytes=50 * MIB),
    )(owners, pieces, *in_hbm(*weights))


def join_kernel(place_ref, back_ref, joined_ref, weight_ref):
    total = jnp.dot(place_ref[...], back_ref[...], preferred_element_type=F32).reshape(8, 8, LANES)
    for start, lanes in ((0, LANES), (4, TOK - LANES)):
        weight = total[start + 3, :, :lanes]
        cols = slice(start * 32, start * 32 + lanes)
        below = jnp.maximum(weight, 1.0)
        for axis in range(3):
            joined_ref[axis, :, cols] = total[start + axis, :, :lanes] / below
        weight_ref[:, cols] = weight


def join(place, back):
    return pl.pallas_call(
        join_kernel,
        in_specs=[VMEM, VMEM],
        out_specs=(VMEM, VMEM),
        out_shape=(
            jax.ShapeDtypeStruct((3, 8, TOK), F32),
            jax.ShapeDtypeStruct((8, TOK), F32),
        ),
        compiler_params=pltpu.CompilerParams(vmem_limit_bytes=8 * MIB),
    )(place, back)


def local(
    tokens,
    image_row,
    views,
    pairs,
    pair_count,
    w_query,
    w_key,
    w_value,
    w_out,
    head_in,
    head_mid,
    head_last,
):
    own = lax.axis_index("img")
    core = lax.axis_index("mdl")

    outgoing = spread(pairs[0].T, tokens.transpose(1, 0, 2)).reshape(64, 8, 14 * LANES)
    pieces = lax.all_to_all(outgoing, "img", split_axis=0, concat_axis=0, tiled=True)

    swap = lambda a: lax.ppermute(a, "mdl", [(0, 1), (1, 0)])
    q_other, k_other, v_other, o_other, h_other = (
        swap(a) for a in (w_query, w_key, w_value, w_out, head_in)
    )
    low = core == 0
    hin0 = jnp.where(low, head_in, h_other)
    hin1 = jnp.where(low, h_other, head_in)

    is_image = views[:, :, None] == jnp.arange(image_row.shape[0])
    stored = jnp.sum(jnp.where(is_image, image_row, 0), axis=2)
    stored_lanes = jnp.pad(stored.astype(F32), ((0, 0), (0, 48)))
    stored_lanes = jnp.concatenate([stored_lanes, stored_lanes], axis=1).reshape(64, 1, LANES)

    chosen = select(pieces.reshape(512, 14 * LANES), stored_lanes)
    arrived = lax.all_to_all(
        chosen.reshape(128, 8, STEPS * LANES),
        ("img", "mdl"),
        split_axis=0,
        concat_axis=0,
        tiled=True,
    )

    my_stored = lax.dynamic_index_in_dim(stored, own, 0, keepdims=False)
    my_views = lax.dynamic_slice_in_dim(pairs.reshape(16), 8 * core, 8, 0)
    my_rows = jnp.sum(jnp.where(my_views[:, None] == jnp.arange(16), my_stored, 0), axis=1)
    live = 4 * core + jnp.arange(8) // 2 < pair_count[0]
    sums = pair_heads(
        jnp.where(live, my_rows // 8, 64),
        arrived.reshape(16, 4, 2, 8, STEPS * LANES),
        (w_query, w_key, w_value, q_other, k_other, v_other, w_out, o_other, hin0, hin1, head_mid, head_last),
    )

    back = lax.all_to_all(
        sums.reshape(128, 8, LANES), ("img", "mdl"), split_axis=0, concat_axis=0, tiled=True
    )
    mine = own * 8 + jnp.arange(8)
    named = jnp.any(stored[None, :, :] == mine[:, None, None], axis=2)
    place = jnp.eye(8, dtype=bool)[:, None, None, None, :] & named[None, :, :, None, None]
    place = jnp.broadcast_to(place, (8, 8, 64, 2, 8)).astype(BF).reshape(64, 1024)
    joined, weight_total = join(place, back.reshape(1024, LANES))
    return (joined.transpose(1, 0, 2), weight_total)


def solution(mesh):
    placed = (
        P("img", None, "mdl"),
        P(),
        P(),
        P("img", None, None),
        P("img"),
        P(None, "mdl"),
        P(None, "mdl"),
        P(None, "mdl"),
        P("mdl", None),
        P("mdl", None),
        P(),
        P(),
    )
    return jax.shard_map(
        local,
        mesh=mesh,
        in_specs=placed,
        out_specs=(P("img", None, None), P("img", None)),
        check_vma=False,
    )
```

```python
import jax
import jax.numpy as jnp
from jax import lax
from jax.experimental import pallas as pl
from jax.experimental.pallas import tpu as pltpu
from jax.sharding import PartitionSpec as P

D = 1024
HALF = 512
HEAD_DIM = 64
TOK = 196
STEPS = 13
PAD_TOK = 208
ROWS = 2 * PAD_TOK
LANES = 128
AHEAD = 1
BODY = 12 * LANES
WAITS = {0: (0, 1), 1: (1, 3), 3: (3, 6)}
SELECT_PARTS = ((0, 384), (384, 704), (704, 896), (896, 1024))
SPREAD_PARTS = tuple((low, min(low + 2, STEPS)) for low in range(0, STEPS, 2))
BF = jnp.bfloat16
F32 = jnp.float32
MIB = 1 << 20
HBM = pl.BlockSpec(memory_space=pltpu.HBM)
VMEM = pl.BlockSpec(memory_space=pltpu.VMEM)
SMEM = pl.BlockSpec(memory_space=pltpu.SMEM)


def iota(shape, axis):
    return lax.broadcasted_iota(jnp.int32, shape, axis)


def spread_kernel(pairs_ref, tokens_ref, out_ref, pairs, tokens, spread_rows, pairs_sem, in_sem, out_sem):
    get_pairs = pltpu.make_async_copy(pairs_ref, pairs, pairs_sem)
    arrive, leave = [], []
    for part, (low, high) in enumerate(SPREAD_PARTS):
        mine = slice(16 * low, min(16 * high, TOK))
        arrive.append(pltpu.make_async_copy(tokens_ref.at[mine], tokens.at[mine], in_sem.at[part]))
        lanes = slice(low * LANES, high * LANES)
        leave.append(
            pltpu.make_async_copy(
                spread_rows.at[:, :, :, lanes], out_ref.at[:, :, :, lanes], out_sem.at[part]
            )
        )
        arrive[part].start()
    get_pairs.start()
    for part, (low, high) in enumerate(SPREAD_PARTS):
        arrive[part].wait()
        for step in range(low, min(high, STEPS - 1)):
            lanes = slice(step * LANES, (step + 1) * LANES)
            for group in range(4):
                spread_rows[:, group, :, lanes] = tokens[
                    16 * step : 16 * step + 16, :, group * LANES : (group + 1) * LANES
                ]
        if high == STEPS:
            get_pairs.wait()
            row, place = iota((8, HALF), 0), (iota((8, HALF), 1) >> 5) & 3
            listed = [jnp.zeros((8, HALF), F32)] * 2
            for entry in range(16):
                value = pairs[entry % 2, entry // 2].astype(F32)
                listed[entry // 8] = jnp.where(row == entry % 8, value, listed[entry // 8])
            lanes = slice((STEPS - 1) * LANES, STEPS * LANES)
            for group in range(16):
                token, block = divmod(group, 4)
                last = jnp.where(place == (block + 2) % 4, listed[1], 0.0)
                last = jnp.where(place == (block + 1) % 4, listed[0], last)
                last = jnp.where(place == block, tokens[16 * (STEPS - 1) + token].astype(F32), last)
                last = last.astype(BF)
                for feature in range(4):
                    spread_rows[group, feature, :, lanes] = last[:, feature * LANES : (feature + 1) * LANES]
        leave[part].start()
    for copy in leave:
        copy.wait()


def in_hbm(*arrays):
    return [pltpu.with_memory_space_constraint(a, pltpu.HBM) for a in arrays]


def spread(pairs, tokens):
    shape = (16, 4, 8, STEPS * LANES)
    return pl.pallas_call(
        spread_kernel,
        in_specs=[HBM, HBM],
        out_specs=HBM,
        out_shape=pltpu.HBM(shape, BF),
        scratch_shapes=[
            pltpu.SMEM((2, 8), jnp.int32),
            pltpu.VMEM((TOK, 8, HALF), BF),
            pltpu.VMEM(shape, BF),
            pltpu.SemaphoreType.DMA,
            pltpu.SemaphoreType.DMA((len(SPREAD_PARTS),)),
            pltpu.SemaphoreType.DMA((len(SPREAD_PARTS),)),
        ],
        compiler_params=pltpu.CompilerParams(vmem_limit_bytes=24 * MIB),
    )(*in_hbm(pairs, tokens))


def select_kernel(block_ref, pieces_ref, stored_ref, out_ref, chosen, sems):
    block = block_ref[0]
    last = pieces_ref[:, BODY:]
    listed = last.astype(F32).reshape(64, 8, LANES)
    lane = iota((64, 8, LANES), 2)
    place = (lane >> 5) & 3
    image = jnp.where(listed == (lane & 31).astype(F32), stored_ref[...], 0.0)
    low = jnp.sum(jnp.where(place == ((block + 1) & 3), image, 0.0), axis=2, keepdims=True)
    high = jnp.sum(jnp.where(place == ((block + 2) & 3), image, 0.0), axis=2, keepdims=True)
    is_token = (iota((512, LANES), 1) >> 5) == block
    last = jnp.where(is_token, last.astype(F32), 0.0).astype(BF)
    rows = jnp.concatenate([low[:, None], high[:, None]], axis=1).reshape(1024, 1)
    leave = []
    for part, (begin, end) in enumerate(SELECT_PARTS):
        mine = slice(begin, end)
        hit = rows[mine] == iota((end - begin, 512), 1).astype(F32)
        hit = jnp.where(hit, 1.0, 0.0).astype(BF)
        got = jnp.dot(hit, pieces_ref[:, :BODY], preferred_element_type=F32)
        chosen[mine, :BODY] = got.astype(BF)
        chosen[mine, BODY:] = jnp.dot(hit, last, preferred_element_type=F32).astype(BF)
        leave.append(pltpu.make_async_copy(chosen.at[mine], out_ref.at[mine], sems.at[part]))
        leave[part].start()
    for copy in leave:
        copy.wait()


def select(block, pieces, stored):
    shape = (1024, STEPS * LANES)
    return pl.pallas_call(
        select_kernel,
        in_specs=[SMEM, VMEM, VMEM],
        out_specs=HBM,
        out_shape=pltpu.HBM(shape, BF),
        scratch_shapes=[pltpu.VMEM(shape, BF), pltpu.SemaphoreType.DMA((len(SELECT_PARTS),))],
        compiler_params=pltpu.CompilerParams(vmem_limit_bytes=24 * MIB),
    )(block, pieces, stored)


def pair_kernel(owner_ref, pieces_ref, *refs):
    sources, out_ref = refs[:12], refs[12]
    weights = refs[13:25]
    x_ref, q_ref, k_ref, v_ref, att_ref, total_ref, send_ref, in_sem, out_sem = refs[25:]
    wo0, wo1, hin0, hin1, hmid, hlast = weights[6:]
    arrive = [
        pltpu.make_async_copy(source, weight, in_sem.at[i])
        for i, (source, weight) in enumerate(zip(sources, weights))
    ]
    for copy in arrive[:6]:
        copy.start()

    out_row = iota((128, 128), 0)
    source = (out_row & 15) * 8 + (out_row >> 4)
    in_row = iota((128, 128), 1)
    perm = jnp.where(source == in_row, 1.0, 0.0).astype(BF)
    is_part = ((in_row & 7) == (out_row >> 4)) & ((in_row >> 5) == (out_row & 15))
    perm_last = jnp.where(is_part, 1.0, 0.0).astype(BF)
    for step in range(STEPS):
        lanes = slice(step * LANES, (step + 1) * LANES)
        columns = []
        for core in range(2):
            for group in range(4):
                tile = pieces_ref[:, group, core, :, lanes].astype(F32)
                columns.append(tile.reshape(128, LANES).astype(BF))
        order = perm if step < STEPS - 1 else perm_last
        moved = jnp.dot(order, jnp.concatenate(columns, axis=1), preferred_element_type=F32)
        x_ref[:, step * 16 : step * 16 + 16, :] = moved.astype(BF).reshape(8, 16, D)

    total_ref[...] = jnp.zeros_like(total_ref)

    def project(duo, begin=0, end=6):
        x = x_ref[4 * duo : 4 * duo + 4].reshape(2 * ROWS, D)
        for which in range(begin, end):
            half, i = divmod(which, 3)
            cols = slice(half * HALF, (half + 1) * HALF)
            if duo == 0 and which in WAITS:
                for copy in arrive[slice(*WAITS[which])]:
                    copy.wait()
                if which == 1:
                    for copy in arrive[6:]:
                        copy.start()
            got = jnp.dot(x, weights[which][...], preferred_element_type=F32).astype(BF)
            if i == 0:
                got = got * jnp.asarray(HEAD_DIM**-0.5, BF)
            (q_ref, k_ref, v_ref)[i][duo, :, cols] = got
            if i == 1:
                is_pad = iota((16, HALF), 0) >= TOK - 192
                for slot in range(4):
                    start = slot * PAD_TOK
                    tail = slice(start + 192, start + PAD_TOK)
                    key = k_ref[duo, start : start + 16, cols].astype(F32)[0:1]
                    keys = jnp.where(is_pad, key, k_ref[duo, tail, cols].astype(F32))
                    k_ref[duo, tail, cols] = keys.astype(BF)
            yield

    def attend(*pairs):
        first = iota((PAD_TOK, LANES), 1) < HEAD_DIM
        ones = jnp.where(iota((PAD_TOK, LANES), 0) < TOK, 1.0, 0.0).astype(BF)
        block = lambda slot: slice(slot * PAD_TOK, (slot + 1) * PAD_TOK)
        chains = [
            (
                pair // 2,
                block(2 * (pair % 2) + slot),
                block(2 * (pair % 2) + 1 - slot),
                slice(two * LANES, (two + 1) * LANES),
            )
            for pair in pairs
            for two in range(D // LANES)
            for slot in range(2)
        ]
        scores = []
        for turn in range(len(chains) + AHEAD):
            if turn < len(chains):
                duo, mine, other, cols = chains[turn]
                q = q_ref[duo, mine, cols]
                none = jnp.zeros_like(q)
                both = jnp.concatenate([jnp.where(first, q, none), jnp.where(first, none, q)], axis=0)
                scores.append(
                    lax.dot_general(
                        both, k_ref[duo, other, cols], (((1,), (1,)), ((), ())), preferred_element_type=F32
                    )
                )
            if turn >= AHEAD:
                duo, mine, other, cols = chains[turn - AHEAD]
                score = scores[turn - AHEAD]
                weight = jnp.exp(score - jnp.max(score, axis=1, keepdims=True)).astype(BF)
                values = jnp.concatenate([v_ref[duo, other, cols], ones], axis=1)
                got = jnp.dot(weight, values, preferred_element_type=F32)
                top = jnp.where(first, got[:PAD_TOK, :LANES], got[PAD_TOK:, :LANES])
                below = jnp.where(first, got[:PAD_TOK, LANES:], got[PAD_TOK:, LANES:])
                att_ref[duo, mine, cols] = (top / below).astype(BF)

    def head(*pairs):
        count = 2 * len(pairs)
        x = x_ref[2 * pairs[0] : 2 * pairs[0] + count].reshape(count * PAD_TOK, D)
        start = 2 * (pairs[0] % 2) * PAD_TOK
        att = att_ref.at[pairs[0] // 2, start : start + count * PAD_TOK]
        mixed = x.astype(F32) + jnp.dot(att[:, :HALF], wo0[...], preferred_element_type=F32)
        mixed = mixed + jnp.dot(att[:, HALF:], wo1[...], preferred_element_type=F32)
        yield
        mean = jnp.sum(mixed, axis=1, keepdims=True) * (1.0 / D)
        square = jnp.sum(mixed * mixed, axis=1, keepdims=True) * (1.0 / D)
        normed = ((mixed - mean) * lax.rsqrt(square - mean * mean + 1e-05)).astype(BF)
        hidden = jnp.dot(normed[:, :HALF], hin0[...], preferred_element_type=F32)
        hidden = hidden + jnp.dot(normed[:, HALF:], hin1[...], preferred_element_type=F32)
        yield
        hidden = jax.nn.gelu(hidden).astype(BF)
        inner = jnp.dot(hidden, hmid[...], preferred_element_type=F32)
        yield
        inner = jax.nn.gelu(inner).astype(BF)
        for slot in range(count):
            last = lax.dot_general(
                hlast[...],
                inner[slot * PAD_TOK : (slot + 1) * PAD_TOK],
                (((1,), (1,)), ((), ())),
                preferred_element_type=F32,
            )
            logit = last[3:4, :]
            confidence = 1.0 + jnp.maximum(logit, 0.0) + jnp.log1p(jnp.exp(-jnp.abs(logit)))
            result = jnp.where(iota(last.shape, 0) == 3, 1.0, last) * confidence
            owner = owner_ref[2 * pairs[0] + slot]
            total_ref[owner, 0:4, :] += result[:, :LANES]
            total_ref[owner, 4:8, 0 : PAD_TOK - LANES] += result[:, LANES:]

    def run(*stages):
        stages = list(stages)
        while stages:
            stages = [stage for stage in stages if next(stage, stages) is None]

    run(project(0))
    attend(0)
    for copy in arrive[6:]:
        copy.wait()
    run(head(0), project(1, 0, 3))
    attend(1)
    run(head(1), project(1, 3, 6))
    attend(2, 3)
    run(head(2), head(3))
    send_ref[...] = total_ref[0:64].astype(BF)
    leave = [pltpu.make_async_copy(send_ref, out_ref.at[:, to], out_sem.at[to]) for to in range(2)]
    for copy in leave:
        copy.start()
    for copy in leave:
        copy.wait()


def pair_heads(owners, pieces, weights):
    send = (64, 2, 8, LANES)
    return pl.pallas_call(
        pair_kernel,
        in_specs=[SMEM, VMEM] + [HBM] * len(weights),
        out_specs=HBM,
        out_shape=pltpu.HBM(send, BF),
        scratch_shapes=[pltpu.VMEM(a.shape, BF) for a in weights]
        + [pltpu.VMEM((8, PAD_TOK, D), BF)]
        + [pltpu.VMEM((2, 2 * ROWS, D), BF)] * 4
        + [
            pltpu.VMEM((65, 8, LANES), F32),
            pltpu.VMEM((64, 8, LANES), BF),
            pltpu.SemaphoreType.DMA((len(weights),)),
            pltpu.SemaphoreType.DMA((2,)),
        ],
        compiler_params=pltpu.CompilerParams(vmem_limit_bytes=50 * MIB),
    )(owners, pieces, *in_hbm(*weights))


def join_kernel(place_ref, back_ref, joined_ref, weight_ref):
    total = jnp.dot(place_ref[...], back_ref[...], preferred_element_type=F32).reshape(8, 8, LANES)
    for start, lanes in ((0, LANES), (4, TOK - LANES)):
        weight = total[start + 3, :, :lanes]
        cols = slice(start * 32, start * 32 + lanes)
        below = jnp.maximum(weight, 1.0)
        for axis in range(3):
            joined_ref[axis, :, cols] = total[start + axis, :, :lanes] / below
        weight_ref[:, cols] = weight


def join(place, back):
    return pl.pallas_call(
        join_kernel,
        in_specs=[VMEM, VMEM],
        out_specs=(VMEM, VMEM),
        out_shape=(
            jax.ShapeDtypeStruct((3, 8, TOK), F32),
            jax.ShapeDtypeStruct((8, TOK), F32),
        ),
        compiler_params=pltpu.CompilerParams(vmem_limit_bytes=8 * MIB),
    )(place, back)


def local(
    tokens,
    image_row,
    views,
    pairs,
    pair_count,
    w_query,
    w_key,
    w_value,
    w_out,
    head_in,
    head_mid,
    head_last,
):
    own = lax.axis_index("img")
    core = lax.axis_index("mdl")

    outgoing = spread(pairs[0].T, tokens.transpose(1, 0, 2)).reshape(64, 8, STEPS * LANES)
    pieces = lax.all_to_all(outgoing, "img", split_axis=0, concat_axis=0, tiled=True)

    swap = lambda a: lax.ppermute(a, "mdl", [(0, 1), (1, 0)])
    q_other, k_other, v_other, o_other, h_other = (
        swap(a) for a in (w_query, w_key, w_value, w_out, head_in)
    )
    low = core == 0
    hin0 = jnp.where(low, head_in, h_other)
    hin1 = jnp.where(low, h_other, head_in)

    is_image = views[:, :, None] == jnp.arange(image_row.shape[0])
    stored = jnp.sum(jnp.where(is_image, image_row, 0), axis=2)
    stored_lanes = jnp.pad(stored.astype(F32), ((0, 0), (0, 16)))
    stored_lanes = jnp.tile(stored_lanes, (1, 4)).reshape(64, 1, LANES)

    block = (own // 4 % 4).reshape(1)
    chosen = select(block, pieces.reshape(512, STEPS * LANES), stored_lanes)
    arrived = lax.all_to_all(
        chosen.reshape(128, 8, STEPS * LANES),
        ("img", "mdl"),
        split_axis=0,
        concat_axis=0,
        tiled=True,
    )

    my_stored = lax.dynamic_index_in_dim(stored, own, 0, keepdims=False)
    my_views = lax.dynamic_slice_in_dim(pairs.reshape(16), 8 * core, 8, 0)
    my_rows = jnp.sum(jnp.where(my_views[:, None] == jnp.arange(16), my_stored, 0), axis=1)
    live = 4 * core + jnp.arange(8) // 2 < pair_count[0]
    sums = pair_heads(
        jnp.where(live, my_rows // 8, 64),
        arrived.reshape(16, 4, 2, 8, STEPS * LANES),
        (w_query, w_key, w_value, q_other, k_other, v_other, w_out, o_other, hin0, hin1, head_mid, head_last),
    )

    back = lax.all_to_all(
        sums.reshape(128, 8, LANES), ("img", "mdl"), split_axis=0, concat_axis=0, tiled=True
    )
    mine = own * 8 + jnp.arange(8)
    named = jnp.any(stored[None, :, :] == mine[:, None, None], axis=2)
    place = jnp.eye(8, dtype=bool)[:, None, None, None, :] & named[None, :, :, None, None]
    place = jnp.broadcast_to(place, (8, 8, 64, 2, 8)).astype(BF).reshape(64, 1024)
    joined, weight_total = join(place, back.reshape(1024, LANES))
    return (joined.transpose(1, 0, 2), weight_total)


def solution(mesh):
    placed = (
        P("img", None, "mdl"),
        P(),
        P(),
        P("img", None, None),
        P("img"),
        P(None, "mdl"),
        P(None, "mdl"),
        P(None, "mdl"),
        P("mdl", None),
        P("mdl", None),
        P(),
        P(),
    )
    return jax.shard_map(
        local,
        mesh=mesh,
        in_specs=placed,
        out_specs=(P("img", None, None), P("img", None)),
        check_vma=False,
    )
```

```python
import jax
import jax.numpy as jnp
import numpy as np
from jax import lax
from jax.experimental import pallas as pl
from jax.experimental.pallas import tpu as pltpu
from jax.sharding import PartitionSpec as P

D = 1024
HALF = 512
HEAD_DIM = 64
TOK = 196
STEPS = 13
PAD_TOK = 208
ROWS = 2 * PAD_TOK
LANES = 128
AHEAD = 1
BODY = 12 * LANES
WAITS = {0: (0, 1), 1: (1, 3), 3: (3, 6)}
SELECT_PARTS = ((0, 384), (384, 704), (704, 896), (896, 1024))
SPREAD_PARTS = tuple((low, min(low + 2, STEPS)) for low in range(0, STEPS, 2))
BF = jnp.bfloat16
F32 = jnp.float32
MIB = 1 << 20
HBM = pl.BlockSpec(memory_space=pltpu.HBM)
VMEM = pl.BlockSpec(memory_space=pltpu.VMEM)
SMEM = pl.BlockSpec(memory_space=pltpu.SMEM)


def iota(shape, axis):
    return lax.broadcasted_iota(jnp.int32, shape, axis)


def gelu(x):
    root = (2.0 / np.pi) ** 0.5
    return (0.5 * x) * (1.0 + jnp.tanh(x * (root + (0.044715 * root) * (x * x))))


def spread_kernel(pairs_ref, tokens_ref, out_ref, pairs, tokens, spread_rows, pairs_sem, in_sem, out_sem):
    get_pairs = pltpu.make_async_copy(pairs_ref, pairs, pairs_sem)
    arrive, leave = [], []
    for part, (low, high) in enumerate(SPREAD_PARTS):
        mine = slice(16 * low, min(16 * high, TOK))
        arrive.append(pltpu.make_async_copy(tokens_ref.at[mine], tokens.at[mine], in_sem.at[part]))
        lanes = slice(low * LANES, high * LANES)
        leave.append(
            pltpu.make_async_copy(
                spread_rows.at[:, :, :, lanes], out_ref.at[:, :, :, lanes], out_sem.at[part]
            )
        )
        arrive[part].start()
    get_pairs.start()
    for part, (low, high) in enumerate(SPREAD_PARTS):
        arrive[part].wait()
        for step in range(low, min(high, STEPS - 1)):
            lanes = slice(step * LANES, (step + 1) * LANES)
            for group in range(4):
                spread_rows[:, group, :, lanes] = tokens[
                    16 * step : 16 * step + 16, :, group * LANES : (group + 1) * LANES
                ]
        if high == STEPS:
            get_pairs.wait()
            row, place = iota((8, HALF), 0), (iota((8, HALF), 1) >> 5) & 3
            listed = [jnp.zeros((8, HALF), F32)] * 2
            for entry in range(16):
                value = pairs[entry % 2, entry // 2].astype(F32)
                listed[entry // 8] = jnp.where(row == entry % 8, value, listed[entry // 8])
            lanes = slice((STEPS - 1) * LANES, STEPS * LANES)
            for group in range(16):
                token, block = divmod(group, 4)
                last = jnp.where(place == (block + 2) % 4, listed[1], 0.0)
                last = jnp.where(place == (block + 1) % 4, listed[0], last)
                last = jnp.where(place == block, tokens[16 * (STEPS - 1) + token].astype(F32), last)
                last = last.astype(BF)
                for feature in range(4):
                    spread_rows[group, feature, :, lanes] = last[:, feature * LANES : (feature + 1) * LANES]
        leave[part].start()
    for copy in leave:
        copy.wait()


def in_hbm(*arrays):
    return [pltpu.with_memory_space_constraint(a, pltpu.HBM) for a in arrays]


def spread(pairs, tokens):
    shape = (16, 4, 8, STEPS * LANES)
    return pl.pallas_call(
        spread_kernel,
        in_specs=[HBM, HBM],
        out_specs=HBM,
        out_shape=pltpu.HBM(shape, BF),
        scratch_shapes=[
            pltpu.SMEM((2, 8), jnp.int32),
            pltpu.VMEM((TOK, 8, HALF), BF),
            pltpu.VMEM(shape, BF),
            pltpu.SemaphoreType.DMA,
            pltpu.SemaphoreType.DMA((len(SPREAD_PARTS),)),
            pltpu.SemaphoreType.DMA((len(SPREAD_PARTS),)),
        ],
        compiler_params=pltpu.CompilerParams(vmem_limit_bytes=24 * MIB),
    )(*in_hbm(pairs, tokens))


def select_kernel(block_ref, pieces_ref, stored_ref, out_ref, chosen, sems):
    block = block_ref[0]
    last = pieces_ref[:, BODY:]
    listed = last.astype(F32).reshape(64, 8, LANES)
    lane = iota((64, 8, LANES), 2)
    place = (lane >> 5) & 3
    image = jnp.where(listed == (lane & 31).astype(F32), stored_ref[...], 0.0)
    low = jnp.sum(jnp.where(place == ((block + 1) & 3), image, 0.0), axis=2, keepdims=True)
    high = jnp.sum(jnp.where(place == ((block + 2) & 3), image, 0.0), axis=2, keepdims=True)
    is_token = (iota((512, LANES), 1) >> 5) == block
    last = jnp.where(is_token, last.astype(F32), 0.0).astype(BF)
    rows = jnp.concatenate([low[:, None], high[:, None]], axis=1).reshape(1024, 1)
    leave = []
    for part, (begin, end) in enumerate(SELECT_PARTS):
        mine = slice(begin, end)
        hit = rows[mine] == iota((end - begin, 512), 1).astype(F32)
        hit = jnp.where(hit, 1.0, 0.0).astype(BF)
        got = jnp.dot(hit, pieces_ref[:, :BODY], preferred_element_type=F32)
        chosen[mine, :BODY] = got.astype(BF)
        chosen[mine, BODY:] = jnp.dot(hit, last, preferred_element_type=F32).astype(BF)
        leave.append(pltpu.make_async_copy(chosen.at[mine], out_ref.at[mine], sems.at[part]))
        leave[part].start()
    for copy in leave:
        copy.wait()


def select(block, pieces, stored):
    shape = (1024, STEPS * LANES)
    return pl.pallas_call(
        select_kernel,
        in_specs=[SMEM, VMEM, VMEM],
        out_specs=HBM,
        out_shape=pltpu.HBM(shape, BF),
        scratch_shapes=[pltpu.VMEM(shape, BF), pltpu.SemaphoreType.DMA((len(SELECT_PARTS),))],
        compiler_params=pltpu.CompilerParams(vmem_limit_bytes=24 * MIB),
    )(block, pieces, stored)


def pair_kernel(owner_ref, pieces_ref, *refs):
    sources, out_ref = refs[:12], refs[12]
    weights = refs[13:25]
    x_ref, q_ref, k_ref, v_ref, att_ref, total_ref, send_ref, in_sem, out_sem = refs[25:]
    wo0, wo1, hin0, hin1, hmid, hlast = weights[6:]
    arrive = [
        pltpu.make_async_copy(source, weight, in_sem.at[i])
        for i, (source, weight) in enumerate(zip(sources, weights))
    ]
    for copy in arrive[:6]:
        copy.start()

    out_row = iota((128, 128), 0)
    source = (out_row & 15) * 8 + (out_row >> 4)
    in_row = iota((128, 128), 1)
    perm = jnp.where(source == in_row, 1.0, 0.0).astype(BF)
    is_part = ((in_row & 7) == (out_row >> 4)) & ((in_row >> 5) == (out_row & 15))
    perm_last = jnp.where(is_part, 1.0, 0.0).astype(BF)
    for step in range(STEPS):
        lanes = slice(step * LANES, (step + 1) * LANES)
        columns = []
        for core in range(2):
            for group in range(4):
                tile = pieces_ref[:, group, core, :, lanes].astype(F32)
                columns.append(tile.reshape(128, LANES).astype(BF))
        order = perm if step < STEPS - 1 else perm_last
        moved = jnp.dot(order, jnp.concatenate(columns, axis=1), preferred_element_type=F32)
        x_ref[:, step * 16 : step * 16 + 16, :] = moved.astype(BF).reshape(8, 16, D)

    total_ref[...] = jnp.zeros_like(total_ref)

    def project(duo, begin=0, end=6):
        x = x_ref[4 * duo : 4 * duo + 4].reshape(2 * ROWS, D)
        for which in range(begin, end):
            half, i = divmod(which, 3)
            cols = slice(half * HALF, (half + 1) * HALF)
            if duo == 0 and which in WAITS:
                for copy in arrive[slice(*WAITS[which])]:
                    copy.wait()
                if which == 1:
                    for copy in arrive[6:]:
                        copy.start()
            got = jnp.dot(x, weights[which][...], preferred_element_type=F32).astype(BF)
            if i == 0:
                got = got * jnp.asarray(HEAD_DIM**-0.5, BF)
            (q_ref, k_ref, v_ref)[i][duo, :, cols] = got
            if i == 1:
                is_pad = iota((16, HALF), 0) >= TOK - 192
                for slot in range(4):
                    start = slot * PAD_TOK
                    tail = slice(start + 192, start + PAD_TOK)
                    key = k_ref[duo, start : start + 16, cols].astype(F32)[0:1]
                    keys = jnp.where(is_pad, key, k_ref[duo, tail, cols].astype(F32))
                    k_ref[duo, tail, cols] = keys.astype(BF)
            yield

    def attend(*pairs):
        first = iota((PAD_TOK, LANES), 1) < HEAD_DIM
        ones = jnp.where(iota((PAD_TOK, LANES), 0) < TOK, 1.0, 0.0).astype(BF)
        block = lambda slot: slice(slot * PAD_TOK, (slot + 1) * PAD_TOK)
        chains = [
            (
                pair // 2,
                block(2 * (pair % 2) + slot),
                block(2 * (pair % 2) + 1 - slot),
                slice(two * LANES, (two + 1) * LANES),
            )
            for pair in pairs
            for two in range(D // LANES)
            for slot in range(2)
        ]
        scores = []
        for turn in range(len(chains) + AHEAD):
            if turn < len(chains):
                duo, mine, other, cols = chains[turn]
                q = q_ref[duo, mine, cols]
                none = jnp.zeros_like(q)
                both = jnp.concatenate([jnp.where(first, q, none), jnp.where(first, none, q)], axis=0)
                scores.append(
                    lax.dot_general(
                        both, k_ref[duo, other, cols], (((1,), (1,)), ((), ())), preferred_element_type=F32
                    )
                )
            if turn >= AHEAD:
                duo, mine, other, cols = chains[turn - AHEAD]
                score = scores[turn - AHEAD]
                weight = jnp.exp(score - jnp.max(score, axis=1, keepdims=True)).astype(BF)
                values = jnp.concatenate([v_ref[duo, other, cols], ones], axis=1)
                got = jnp.dot(weight, values, preferred_element_type=F32)
                top = jnp.where(first, got[:PAD_TOK, :LANES], got[PAD_TOK:, :LANES])
                below = jnp.where(first, got[:PAD_TOK, LANES:], got[PAD_TOK:, LANES:])
                att_ref[duo, mine, cols] = (top / below).astype(BF)

    def head(*pairs):
        count = 2 * len(pairs)
        x = x_ref[2 * pairs[0] : 2 * pairs[0] + count].reshape(count * PAD_TOK, D)
        start = 2 * (pairs[0] % 2) * PAD_TOK
        att = att_ref.at[pairs[0] // 2, start : start + count * PAD_TOK]
        mixed = x.astype(F32) + jnp.dot(att[:, :HALF], wo0[...], preferred_element_type=F32)
        mixed = mixed + jnp.dot(att[:, HALF:], wo1[...], preferred_element_type=F32)
        yield
        mean = jnp.sum(mixed, axis=1, keepdims=True) * (1.0 / D)
        square = jnp.sum(mixed * mixed, axis=1, keepdims=True) * (1.0 / D)
        normed = ((mixed - mean) * lax.rsqrt(square - mean * mean + 1e-05)).astype(BF)
        hidden = jnp.dot(normed[:, :HALF], hin0[...], preferred_element_type=F32)
        hidden = hidden + jnp.dot(normed[:, HALF:], hin1[...], preferred_element_type=F32)
        yield
        hidden = gelu(hidden).astype(BF)
        inner = jnp.dot(hidden, hmid[...], preferred_element_type=F32)
        yield
        inner = gelu(inner).astype(BF)
        for slot in range(count):
            last = lax.dot_general(
                hlast[...],
                inner[slot * PAD_TOK : (slot + 1) * PAD_TOK],
                (((1,), (1,)), ((), ())),
                preferred_element_type=F32,
            )
            logit = last[3:4, :]
            confidence = 1.0 + jnp.maximum(logit, 0.0) + jnp.log1p(jnp.exp(-jnp.abs(logit)))
            result = jnp.where(iota(last.shape, 0) == 3, 1.0, last) * confidence
            owner = owner_ref[2 * pairs[0] + slot]
            total_ref[owner, 0:4, :] += result[:, :LANES]
            total_ref[owner, 4:8, 0 : PAD_TOK - LANES] += result[:, LANES:]

    def run(*stages):
        stages = list(stages)
        while stages:
            stages = [stage for stage in stages if next(stage, stages) is None]

    run(project(0))
    attend(0)
    for copy in arrive[6:]:
        copy.wait()
    run(head(0), project(1, 0, 3))
    attend(1)
    run(head(1), project(1, 3, 6))
    attend(2, 3)
    run(head(2), head(3))
    send_ref[...] = total_ref[0:64].astype(BF)
    leave = [pltpu.make_async_copy(send_ref, out_ref.at[:, to], out_sem.at[to]) for to in range(2)]
    for copy in leave:
        copy.start()
    for copy in leave:
        copy.wait()


def pair_heads(owners, pieces, weights):
    send = (64, 2, 8, LANES)
    return pl.pallas_call(
        pair_kernel,
        in_specs=[SMEM, VMEM] + [HBM] * len(weights),
        out_specs=HBM,
        out_shape=pltpu.HBM(send, BF),
        scratch_shapes=[pltpu.VMEM(a.shape, BF) for a in weights]
        + [pltpu.VMEM((8, PAD_TOK, D), BF)]
        + [pltpu.VMEM((2, 2 * ROWS, D), BF)] * 4
        + [
            pltpu.VMEM((65, 8, LANES), F32),
            pltpu.VMEM((64, 8, LANES), BF),
            pltpu.SemaphoreType.DMA((len(weights),)),
            pltpu.SemaphoreType.DMA((2,)),
        ],
        compiler_params=pltpu.CompilerParams(vmem_limit_bytes=50 * MIB),
    )(owners, pieces, *in_hbm(*weights))


def join_kernel(place_ref, back_ref, joined_ref, weight_ref):
    total = jnp.dot(place_ref[...], back_ref[...], preferred_element_type=F32).reshape(8, 8, LANES)
    for start, lanes in ((0, LANES), (4, TOK - LANES)):
        weight = total[start + 3, :, :lanes]
        cols = slice(start * 32, start * 32 + lanes)
        below = jnp.maximum(weight, 1.0)
        for axis in range(3):
            joined_ref[axis, :, cols] = total[start + axis, :, :lanes] / below
        weight_ref[:, cols] = weight


def join(place, back):
    return pl.pallas_call(
        join_kernel,
        in_specs=[VMEM, VMEM],
        out_specs=(VMEM, VMEM),
        out_shape=(
            jax.ShapeDtypeStruct((3, 8, TOK), F32),
            jax.ShapeDtypeStruct((8, TOK), F32),
        ),
        compiler_params=pltpu.CompilerParams(vmem_limit_bytes=8 * MIB),
    )(place, back)


def local(
    tokens,
    image_row,
    views,
    pairs,
    pair_count,
    w_query,
    w_key,
    w_value,
    w_out,
    head_in,
    head_mid,
    head_last,
):
    own = lax.axis_index("img")
    core = lax.axis_index("mdl")

    outgoing = spread(pairs[0].T, tokens.transpose(1, 0, 2)).reshape(64, 8, STEPS * LANES)
    pieces = lax.all_to_all(outgoing, "img", split_axis=0, concat_axis=0, tiled=True)

    swap = lambda a: lax.ppermute(a, "mdl", [(0, 1), (1, 0)])
    q_other, k_other, v_other, o_other, h_other = (
        swap(a) for a in (w_query, w_key, w_value, w_out, head_in)
    )
    low = core == 0
    hin0 = jnp.where(low, head_in, h_other)
    hin1 = jnp.where(low, h_other, head_in)

    is_image = views[:, :, None] == jnp.arange(image_row.shape[0])
    stored = jnp.sum(jnp.where(is_image, image_row, 0), axis=2)
    stored_lanes = jnp.pad(stored.astype(F32), ((0, 0), (0, 16)))
    stored_lanes = jnp.tile(stored_lanes, (1, 4)).reshape(64, 1, LANES)

    block = (own // 4 % 4).reshape(1)
    chosen = select(block, pieces.reshape(512, STEPS * LANES), stored_lanes)
    arrived = lax.all_to_all(
        chosen.reshape(128, 8, STEPS * LANES),
        ("img", "mdl"),
        split_axis=0,
        concat_axis=0,
        tiled=True,
    )

    my_stored = lax.dynamic_index_in_dim(stored, own, 0, keepdims=False)
    my_views = lax.dynamic_slice_in_dim(pairs.reshape(16), 8 * core, 8, 0)
    my_rows = jnp.sum(jnp.where(my_views[:, None] == jnp.arange(16), my_stored, 0), axis=1)
    live = 4 * core + jnp.arange(8) // 2 < pair_count[0]
    sums = pair_heads(
        jnp.where(live, my_rows // 8, 64),
        arrived.reshape(16, 4, 2, 8, STEPS * LANES),
        (w_query, w_key, w_value, q_other, k_other, v_other, w_out, o_other, hin0, hin1, head_mid, head_last),
    )

    back = lax.all_to_all(
        sums.reshape(128, 8, LANES), ("img", "mdl"), split_axis=0, concat_axis=0, tiled=True
    )
    mine = own * 8 + jnp.arange(8)
    named = jnp.any(stored[None, :, :] == mine[:, None, None], axis=2)
    place = jnp.eye(8, dtype=bool)[:, None, None, None, :] & named[None, :, :, None, None]
    place = jnp.broadcast_to(place, (8, 8, 64, 2, 8)).astype(BF).reshape(64, 1024)
    joined, weight_total = join(place, back.reshape(1024, LANES))
    return (joined.transpose(1, 0, 2), weight_total)


def solution(mesh):
    placed = (
        P("img", None, "mdl"),
        P(),
        P(),
        P("img", None, None),
        P("img"),
        P(None, "mdl"),
        P(None, "mdl"),
        P(None, "mdl"),
        P("mdl", None),
        P("mdl", None),
        P(),
        P(),
    )
    return jax.shard_map(
        local,
        mesh=mesh,
        in_specs=placed,
        out_specs=(P("img", None, None), P("img", None)),
        check_vma=False,
    )
```
